512 devices in a mesh: band: 128 (over y, z, core), chan: 4 (over x).
Axes of the slice: x: 4, y: 4, z: 16, core: 2. Of those that a mesh axis runs over, the one named last changes fastest.
Arguments:
- spectra: bfloat16 [2, 2, 16384, 1024], P(None, None, 'chan', 'band')
- window_flags: int32 [2, 128], replicated, may hold values 0 or 1
- pair_tiles: int32 [4, 128, 2], P('chan'), may hold values from 0 to 127, as said below
- owners: int32 [4, 128, 1], P('chan'), may hold values from 0 to 127; in each aligned block of 128 rows (0 to 127, 128 to 255, ..., all dimensions but the last counted through in order) at most 2 rows name the same one
- stacks: float32 [4, 256, 512, 128], P('chan', 'band'), may hold values from -3 to 3
Outputs:
- new_stacks: float32 [4, 256, 512, 128], P('chan', 'band')
The draws below stay inside these ranges and needn't reach their ends.
Inputs may be any that keep to these rules, and one draw needn't show every extreme that they name: `pair_tiles`: entry 0 is a tile of the pair's own quarter q (q * 32 to q * 32 + 31) and entry 1 = entry 0 + d: either 0 <= d <= 7, with d even where entry 1 lies in the quarter above, or -7 <= d < 0 with entry 1 in the quarter below and d odd. No two pair tiles of the whole cable join the same two tiles. Every quarter has a pair with d = 7, and every quarter but the first one with d = -7. `owners`: no owner holds more than 2 pair tiles of one quarter; some owner holds exactly 2.
All inputs are finite; a program needn't handle non-finite values.
Results may differ from the reference program's by a relative error of at most 0.0039.
Values may be sent and summed in bfloat16 or wider, within the bound.
A program may use at most 64 MiB of HBM per device.

```python
import math
import jax
import jax.numpy as jnp
import numpy as np
from jax import lax

TILE = 128
MAXOFF = 7
LAGS = 512
CAP = 2
W = 2
F_DEV = 8
QUARTERS = 4
CH = 16384
CH_TILES = 128
TQ = 32
NF = 1024
PAIRS = 128
SLOTS = 256
N_BAND = 128


def draw_spectra(key, part):
    keys = jax.random.split(key, 3)
    shape = (W, 2, CH, NF)
    channel_level = jnp.exp(jax.random.uniform(keys[2], (W, 1, CH, 1)) * math.log(10.0))
    bin_level = jnp.exp(jax.random.uniform(keys[1], (1, 1, 1, NF)) * math.log(10.0))
    values = jax.random.normal(keys[0], shape) * bin_level * channel_level
    return values.astype(jnp.float32).astype(jnp.bfloat16)


def draw_pair_tiles(key, part):
    span = 2 * MAXOFF + 1
    count = TQ * span
    index = jnp.arange(count, dtype=jnp.int32)
    collected = []
    for quarter in range(QUARTERS):
        lowest = quarter * TQ
        source = lowest + index // span
        offset = index % span - MAXOFF
        target = source + offset
        inside = (target >= 0) & (target < CH_TILES)
        upward = (offset >= 0) & ((target < lowest + TQ) | (offset % 2 == 0))
        downward = (offset < 0) & (target < lowest) & (-offset % 2 == 1)
        valid = inside & (upward | downward)
        score = jax.random.permutation(jax.random.fold_in(key, quarter), count).astype(jnp.int32) + 2
        score = jnp.where((source == lowest) & (offset == -MAXOFF), 0, score)
        score = jnp.where((source == lowest) & (offset == MAXOFF), 1, score)
        score = jnp.where(valid, score, score + 4 * count)
        order = jnp.argsort(score, stable=True)[:PAIRS]
        collected.append(jnp.stack([source[order], target[order]], axis=-1))
    return jnp.stack(collected).astype(jnp.int32)


def touch_ends(values, rng, least, top_value):
    shape = values.shape
    spot = [jax.random.randint(jax.random.fold_in(rng, axis), (), 0, shape[axis]) for axis in range(len(shape))]
    values = values.at[tuple(spot)].set(least)
    longest = shape.index(max(shape))
    spot[longest] = (spot[longest] + 1) % shape[longest]
    return values.at[tuple(spot)].set(top_value)


def levels(stream_key, extent, cuts, least, top_value):
    def one(dim, parts):
        steps = jax.random.uniform(jax.random.fold_in(jax.random.fold_in(stream_key, 6), dim), (parts,), jnp.float32, least / len(cuts), top_value / len(cuts))
        return jnp.repeat(jnp.exp(steps), extent[dim] // parts).reshape((-1,) + (1,) * (len(extent) - dim - 1))

    factor_of = one(*cuts[0])
    for cut in cuts[1:]:
        factor_of = factor_of * one(*cut)
    return factor_of


def shared_out(key, own, number, rows, number_of, top, bound, lean):
    ranking = jax.random.permutation(key, number_of)
    packed, usual = portions_of(number_of, rows * top, bound, lean, True), portions_of(number_of, rows * top, bound, lean, False)
    places = jnp.arange(number_of)

    def named(tallies, rotation):
        used = int((tallies > 0).sum())
        fixed = max(1, used // 4)
        moved = fixed + (places - fixed + rotation * (used - fixed)) % max(1, number_of - fixed)
        return jnp.zeros((number_of,), jnp.int32).at[ranking[jnp.where(places < fixed, places, moved)]].set(jnp.asarray(tallies, jnp.int32))

    tallies = jnp.where(number % 4 == 0, named(packed, number // 4), named(usual, number - number // 4 - 1))
    mixed = jax.random.permutation(jax.random.fold_in(own, 3), number_of)
    donor, taker = mixed[0:number_of // 2 * 2:2], mixed[1:number_of // 2 * 2:2]
    margin = jnp.minimum(tallies[donor] - 1, bound - tallies[taker]) // 2
    margin = jnp.where((donor == ranking[0]) | (taker == ranking[0]) | (tallies[taker] == 0), 0, jnp.maximum(margin, 0))
    moved = jax.random.randint(jax.random.fold_in(own, 4), (number_of // 2,), 0, 1 << 20) % (margin + 1)
    tallies = tallies.at[donor].add(-moved).at[taker].add(moved)
    members = jnp.searchsorted(jnp.cumsum(tallies), jnp.arange(rows * top), side="right").astype(jnp.int32)
    listing = members.reshape(top, rows).T
    listing = listing[jax.random.permutation(jax.random.fold_in(own, 1), rows)]
    rotation = jax.random.randint(jax.random.fold_in(own, 2), (rows, 1), 0, top)
    return jnp.take_along_axis(listing, (jnp.arange(top)[None, :] + rotation) % top, axis=1)


def portions_of(number_of, total, reach, slope, full):
    loads = [(1 << 20) // math.isqrt(standing ** slope) + 1 for standing in range(1, number_of + 1)]
    largest = reach if full else min(reach, max(-(-total // number_of), total * loads[0] // sum(loads)))
    least = 1 if total - largest >= number_of - 1 else 0
    holding, rest = [largest] + [least] * (number_of - 1), total - largest - least * (number_of - 1)
    while rest > 0:
        movable = [i for i in range(1, number_of) if holding[i] < largest] or [i for i in range(1, number_of) if holding[i] < reach]
        mass, remaining = sum([loads[i] for i in movable]), rest
        for i in movable:
            extra = min(reach - holding[i], max(1, remaining * loads[i] // mass), rest)
            holding[i] = holding[i] + extra
            rest = rest - extra
    return np.array(holding)


def gaussian(stream_key, dims, deviation, most, cuts=(), kind=jnp.bfloat16):
    values = deviation * jax.random.normal(stream_key, dims, jnp.float32)
    if cuts:
        values = values * levels(stream_key, dims, cuts, -0.22, 0.18)
    return jnp.clip(values, -most, most).astype(kind)


def setup_inputs(seed: int = 0) -> dict:
    arg_keys = jax.random.split(jax.random.key(seed), 6)
    spectra = draw_spectra(jax.random.fold_in(arg_keys[5], 71), 0)
    window_flags = touch_ends((jax.random.randint(arg_keys[1], (W, CH_TILES), 0, 4) < 3).astype(jnp.int32), jax.random.fold_in(arg_keys[1], 1), 0, 1)
    pair_tiles = draw_pair_tiles(jax.random.fold_in(arg_keys[5], 71), 0)
    owners_keys = jax.random.split(jax.random.fold_in(arg_keys[3], 1), QUARTERS * PAIRS // PAIRS)
    owners_turns = jax.random.permutation(jax.random.fold_in(arg_keys[3], 3), QUARTERS * PAIRS // PAIRS)
    owners = jax.vmap(lambda own, number: shared_out(jax.random.fold_in(arg_keys[3], 2), own, number, PAIRS, N_BAND, 1, CAP, 2))(owners_keys, owners_turns).reshape((QUARTERS, PAIRS, 1))
    stacks = gaussian(arg_keys[4], (QUARTERS, SLOTS, LAGS, TILE), 0.5, 3.0, ((0, 4), (1, 128)), jnp.float32)
    return {"spectra": spectra, "window_flags": window_flags, "pair_tiles": pair_tiles, "owners": owners, "stacks": stacks}


STABILITY_FLOOR = 1e-05

def lag_table(first_bin, bin_count, total_bins):
    frequency = first_bin + lax.iota(jnp.int32, bin_count)
    lag_shift = lax.iota(jnp.int32, LAGS) - LAGS // 2
    phase_index = jnp.mod(lag_shift[:, None] * frequency[None, :], total_bins)
    angles = phase_index.astype(jnp.float32) * (2.0 * math.pi / total_bins)
    amplitude = 1.0 / math.sqrt(total_bins)
    return jnp.concatenate([jnp.cos(angles) * amplitude, -jnp.sin(angles) * amplitude], axis=1).astype(jnp.bfloat16)

def whiten_window(spectrum, tile_validity_flags):
    values = spectrum.astype(jnp.float32)
    energy = values[0] * values[0] + values[1] * values[1]
    block_list = energy.reshape(CH, N_BAND, F_DEV)
    level = jnp.sqrt(lax.optimization_barrier(jnp.mean(block_list, axis=-1)) + STABILITY_FLOOR)
    level = jnp.repeat(level, F_DEV, axis=1)
    gate = jnp.repeat(tile_validity_flags.astype(jnp.float32), TILE)
    return (values / level[None] * gate[None, :, None]).astype(jnp.bfloat16)

def pair_lags(left_tiles, right_tiles, divisor, lag_weights):
    left_real = left_tiles[:, 0].astype(jnp.float32)
    left_imag = left_tiles[:, 1].astype(jnp.float32)
    right_real = right_tiles[:, 0].astype(jnp.float32)
    right_imag = right_tiles[:, 1].astype(jnp.float32)
    real_part = lax.optimization_barrier(jnp.sum(left_real * right_real + left_imag * right_imag, axis=0))
    imaginary_component = lax.optimization_barrier(jnp.sum(left_real * right_imag - left_imag * right_real, axis=0))
    spectrum = (jnp.concatenate([real_part, imaginary_component], axis=-1) / divisor).astype(jnp.bfloat16)
    return jnp.dot(lag_weights.astype(jnp.float32), spectrum.astype(jnp.float32).T, precision=lax.Precision.HIGHEST)

def reference(spectra, window_flags, pair_tiles, owners, stacks):

    def whiten_item(item):
        return whiten_window(item[0], item[1])
    whitened = lax.map(whiten_item, (spectra, window_flags))
    lag_weights = lag_table(0, NF, NF)
    result = stacks
    position = lax.iota(jnp.int32, PAIRS)
    for quarter in range(QUARTERS):
        pair_list = pair_tiles[quarter]
        owner_ids = owners[quarter, :, 0]

        def one_pair(entry):
            source = entry[0]
            target = entry[1]
            left_tiles = lax.dynamic_slice_in_dim(whitened, source * TILE, TILE, 2)
            right_tiles = lax.dynamic_slice_in_dim(whitened, target * TILE, TILE, 2)
            together = jnp.sum(window_flags[:, source] * window_flags[:, target])
            divisor = jnp.maximum(together, 1).astype(jnp.float32)
            return pair_lags(left_tiles, right_tiles, divisor, lag_weights)
        every_lag_value = lax.map(one_pair, pair_list)
        earlier = (owner_ids[:, None] == owner_ids[None, :]) & (position[None, :] < position[:, None])
        slot_rank = lax.optimization_barrier(jnp.sum(earlier.astype(jnp.int32), axis=1))
        slot_index = owner_ids * CAP + slot_rank
        result = result.at[quarter, slot_index].add(every_lag_value)
    return result
```

```python
import math

import jax
import jax.numpy as jnp
import numpy as np
from jax import lax
from jax.experimental import pallas as pl
from jax.experimental.pallas import tpu as pltpu
from jax.sharding import PartitionSpec as P

TILE = 128
LAGS = 512
NF = 1024
NY, NZ = 4, 16
CHIPS = NY * NZ
QUARTERS = 4
TQ = 32
BINS = 8
FLOOR = 1e-05
BF = jnp.bfloat16
F32 = jnp.float32


def lag_table():
    tau = np.arange(LAGS) - LAGS // 2
    phase = np.mod(tau[:, None] * np.arange(NF)[None, :], NF)
    angles = phase.astype(np.float32) * np.float32(2.0 * math.pi / NF)
    amplitude = np.float32(1.0 / math.sqrt(NF))
    both = np.stack([np.cos(angles) * amplitude, -np.sin(angles) * amplitude])
    both = both.astype(np.float32).astype(jnp.bfloat16)
    both = both.reshape(2, LAGS, NY, NZ, 2, BINS)
    return both.transpose(2, 4, 1, 0, 3, 5).reshape(NY * 2, LAGS, 2 * NZ * BINS)


def place(tile, part):
    if tile < 8:
        return part * 8 + tile
    if tile < 24:
        return 32 + part * 16 + tile - 8
    return 96 + part * 8 + tile - 24


def send(src, dst, send_sem, recv_sem, where):
    pltpu.make_async_remote_copy(
        src_ref=src,
        dst_ref=dst,
        send_sem=send_sem,
        recv_sem=recv_sem,
        device_id=where,
        device_id_type=pl.DeviceIdType.MESH,
    ).start()


def wait_for(ref, sem):
    pltpu.make_async_copy(ref, ref, sem).wait()


def selection(quarter, core, fl_ref, pt_ref, ow_ref, s_mat):
    ii = lax.broadcasted_iota(jnp.int32, (TILE, TILE), 0)
    jj = lax.broadcasted_iota(jnp.int32, (TILE, TILE), 1)

    def row(values):
        return jnp.broadcast_to(values.astype(F32), (TILE, TILE))

    own = row(ow_ref[...])
    own_c = own.T
    rank = jnp.sum(jnp.where((own_c == own) & (jj < ii), 1.0, 0.0), axis=1, keepdims=True)
    holder = (2 * (jj % CHIPS) + core).astype(F32)
    order = (jj // CHIPS).astype(F32)
    chosen = jnp.where((own_c == holder) & (rank == order), 1.0, 0.0)
    a = jnp.sum(chosen * (row(pt_ref[0:1, :]).T + 1.0), axis=0, keepdims=True) - 1.0
    t = jnp.sum(chosen * (row(pt_ref[1:2, :]).T + 1.0), axis=0, keepdims=True) - 1.0
    tiles = ii.astype(F32)
    flags_a, flags_t = [], []
    for w in range(2):
        fc = row(fl_ref[w : w + 1, :]).T
        flags_a.append(jnp.sum(jnp.where(tiles == a, fc, 0.0), axis=0, keepdims=True))
        flags_t.append(jnp.sum(jnp.where(tiles == t, fc, 0.0), axis=0, keepdims=True))
    together = flags_a[0] * flags_t[0] + flags_a[1] * flags_t[1]
    share = jnp.where(together > 1.5, 0.5, 1.0)
    first = (quarter * TQ).astype(F32)
    a_here = a - first
    t_here = t - first
    low, mid = ii < 32, ii < 96
    part = jnp.where(low, ii // 8, jnp.where(mid, (ii - 32) // 16, (ii - 96) // 8))
    tile = jnp.where(low, ii % 8, jnp.where(mid, 8 + ii % 16, 24 + ii % 8)).astype(F32)
    edge_part = jnp.where(low, ii // 8, jnp.where(ii < 64, (ii - 32) // 8, -1))
    edge_tile = jnp.where(low, ii % 8 - 8, 32 + ii % 8).astype(F32)
    for p in range(4):
        w = p // 2
        left = pl.ds(p * TILE, TILE)
        right = pl.ds((4 + p) * TILE, TILE)
        here = part == p
        s_mat[0:TILE, left] = jnp.where(
            here & (tile == a_here), flags_a[w] * share, 0.0
        ).astype(BF)
        s_mat[0:TILE, right] = jnp.where(here & (tile == t_here), flags_t[w], 0.0).astype(BF)
        s_mat[TILE : 2 * TILE, left] = jnp.zeros((TILE, TILE), BF)
        s_mat[TILE : 2 * TILE, right] = jnp.where(
            (edge_part == p) & (edge_tile == t_here), flags_t[w], 0.0
        ).astype(BF)


def kernel(
    x_hbm, fl_hbm, pt_hbm, ow_hbm, w_hbm, out_ref,
    x_v, fl_v, pt_v, ow_v, w_v, a_f, b_f, b_h, r, hs, h, s_mat, acc, y_h, q_h,
    in_sems, w_sem, send1, recv1, sib_send, sib_recv, edge_send, edge_recv, send2, recv2,
):
    band = lax.axis_index("band")
    quarter = lax.axis_index("chan")
    chip, core = band // 2, band % 2
    y, z = chip // NZ, chip % NZ
    other = chip * 2 + 1 - core
    up = (quarter + 1) % QUARTERS
    down = (quarter + QUARTERS - 1) % QUARTERS

    loads = [
        pltpu.make_async_copy(x_hbm, x_v, in_sems.at[0]),
        pltpu.make_async_copy(fl_hbm, fl_v, in_sems.at[1]),
        pltpu.make_async_copy(pt_hbm, pt_v, in_sems.at[2]),
        pltpu.make_async_copy(ow_hbm, ow_v, in_sems.at[3]),
    ]
    for load in loads:
        load.start()
    load_w = pltpu.make_async_copy(w_hbm, w_v, w_sem)
    load_w.start()

    barrier = pltpu.get_barrier_semaphore()

    def greet(to_band, to_chan):
        pl.semaphore_signal(
            barrier, inc=1, device_id=(to_band, to_chan), device_id_type=pl.DeviceIdType.MESH
        )

    @pl.loop(1, CHIPS)
    def _(i):
        greet(((chip + i) % CHIPS) * 2 + core, quarter)

    greet(other, quarter)
    for beside in (up, down):
        greet(band, beside)
        greet(other, beside)

    for load in loads:
        load.wait()

    for tile in range(TQ):
        lanes = pl.ds(tile * TILE, TILE)
        for w in range(2):
            re = x_v[2 * w, :, lanes].astype(F32)
            im = x_v[2 * w + 1, :, lanes].astype(F32)
            energy = jnp.sum(re * re + im * im, axis=0, keepdims=True)
            scale = lax.rsqrt(energy * (1.0 / BINS) + FLOOR)
            a_f[pl.ds(8 * place(tile, 2 * w), 8), :] = re * scale
            a_f[pl.ds(8 * place(tile, 2 * w + 1), 8), :] = im * scale
    for i in range(BINS):
        b_f[pl.ds(i, TILE, stride=BINS), :] = a_f[pl.ds(i, TILE, stride=BINS), :].T
    b_h[...] = b_f[...].astype(BF).reshape(CHIPS, 16, TILE)

    pl.semaphore_wait(barrier, CHIPS - 1 + 5)

    def exchange(src, dst, send_sem, recv_sems):
        for t in (1, 2, 3, 0):
            row = (y + t) % NY

            @pl.loop(1 if t == 0 else 0, NZ)
            def _(i):
                g = row * NZ + (z + i) % NZ
                send(
                    src.at[g], dst.at[chip], send_sem, recv_sems.at[t],
                    (g * 2 + core, quarter),
                )

        pltpu.make_async_copy(src.at[chip], dst.at[chip], recv_sems.at[0]).start()

    exchange(b_h, r.at[0], send1, recv1)

    selection(quarter, core, fl_v, pt_v, ow_v, s_mat)
    acc[...] = jnp.zeros_like(acc)
    load_w.wait()

    block = lax.broadcasted_iota(jnp.int32, (64, TILE), 1) // 32

    def arrive(t):
        chips = pl.ds(((y + NY - t) % NY) * NZ, NZ)
        wait_for(r.at[0, chips], recv1.at[t])
        send(r.at[0, chips], r.at[1, chips], sib_send, sib_recv.at[t], (other, quarter))
        rows = r[0, chips].reshape(4, 64, TILE).astype(F32)
        high = rows[3]
        low = rows[0]
        for q in range(3):
            high = jnp.where(block == q, pltpu.roll(rows[q], (32 * q + 32) % TILE, 1), high)
        for q in range(1, 4):
            low = jnp.where(block == q, pltpu.roll(rows[q], 32 * q, 1), low)
        hs[t, 0] = high.astype(BF)
        hs[t, 1] = low.astype(BF)
        for d, beside in ((0, up), (1, down)):
            send(hs.at[t, d], h.at[t, 0, d], edge_send, edge_recv.at[t], (band, beside))
            send(hs.at[t, d], h.at[t, 1, d], edge_send, edge_recv.at[t], (other, beside))

    def compute(t):
        row = (y + NY - t) % NY
        chips = pl.ds(row * NZ, NZ)
        wait_for(h.at[t], edge_recv.at[t])
        wait_for(r.at[1, chips], sib_recv.at[t])
        total = None
        for o in range(2):
            from_low = h[t, o, 0].astype(F32)
            from_high = h[t, o, 1].astype(F32)
            edge = jnp.concatenate(
                [
                    jnp.where(
                        block == 0,
                        pltpu.roll(from_low, (TILE - 32 * q) % TILE, 1) if q else from_low,
                        pltpu.roll(from_high, (TILE + 32 - 32 * q) % TILE, 1)
                        if q != 1
                        else from_high,
                    )
                    for q in range(4)
                ],
                axis=0,
            ).astype(BF)
            rows = jnp.concatenate([r[o, chips].reshape(2 * TILE, TILE), edge], axis=1)
            g = jnp.dot(rows, s_mat[...], preferred_element_type=F32)
            left = [g[:, p * TILE : (p + 1) * TILE] for p in range(4)]
            right = [g[:, (4 + p) * TILE : (5 + p) * TILE] for p in range(4)]
            re = (left[0] * right[0] + left[1] * right[1]) + (
                left[2] * right[2] + left[3] * right[3]
            )
            im = (left[0] * right[1] - left[1] * right[0]) + (
                left[2] * right[3] - left[3] * right[2]
            )
            re = re.reshape(NZ, 2, BINS, TILE)
            im = im.reshape(NZ, 2, BINS, TILE)
            cross = jnp.concatenate(
                [
                    jnp.concatenate(
                        [v[:, k].reshape(TILE, TILE).astype(BF) for k in range(2)], axis=1
                    )
                    for v in (re, im)
                ],
                axis=0,
            )
            index = row * 2 + (core if o == 0 else 1 - core)
            part = jnp.dot(w_v[index], cross, preferred_element_type=F32)
            total = part if total is None else total + part
        acc[...] += total

    arrive(1)

    @pl.loop(2, 4)
    def _(t):
        arrive(t)
        compute(t - 1)

    arrive(0)
    compute(3)
    compute(0)

    for k in range(2):
        for c in range(4):
            turned = acc[c * TILE : (c + 1) * TILE, k * TILE : (k + 1) * TILE].T
            for s in range(2):
                b_f[pl.ds(k * 8 + s * 4 + c, CHIPS, stride=16), :] = turned[
                    s * CHIPS : (s + 1) * CHIPS
                ]
    y_h[...] = b_f[...].astype(BF).reshape(CHIPS, 16, TILE)
    exchange(y_h, q_h, send2, recv2)

    for t in (1, 2, 3, 0):
        row = (y + NY - t) % NY
        chips = pl.ds(row * NZ, NZ)
        wait_for(q_h.at[chips], recv2.at[t])
        a_f[pl.ds(row * 256, 256), :] = q_h[chips].astype(F32).reshape(256, TILE)
    for s in range(2):
        for c in range(4):
            out_ref[s, c * TILE : (c + 1) * TILE, :] = a_f[
                pl.ds(s * 4 + c, TILE, stride=BINS), :
            ].T

    most = pl.ds(0, CHIPS - 1)
    wait_for(b_h.at[most], send1)
    wait_for(y_h.at[most], send2)
    wait_for(r.at[0], sib_send)
    wait_for(h, edge_send)


def body(spectra, window_flags, pair_tiles, owners, stacks):
    x = jnp.transpose(spectra, (0, 1, 3, 2)).reshape(4, BINS, TQ * TILE)
    pairs = pair_tiles[0].T
    held = owners[0].T
    table = jnp.asarray(lag_table())
    dma = pltpu.SemaphoreType.DMA
    added = pl.pallas_call(
        kernel,
        out_shape=jax.ShapeDtypeStruct((2, LAGS, TILE), F32),
        in_specs=[pl.BlockSpec(memory_space=pltpu.HBM)] * 5,
        out_specs=pl.BlockSpec(memory_space=pltpu.VMEM),
        scratch_shapes=[
            pltpu.VMEM((4, BINS, TQ * TILE), BF),
            pltpu.VMEM((2, TILE), jnp.int32),
            pltpu.VMEM((2, TILE), jnp.int32),
            pltpu.VMEM((1, TILE), jnp.int32),
            pltpu.VMEM((NY * 2, LAGS, 256), BF),
            pltpu.VMEM((1024, TILE), F32),
            pltpu.VMEM((1024, TILE), F32),
            pltpu.VMEM((CHIPS, 16, TILE), BF),
            pltpu.VMEM((2, CHIPS, 16, TILE), BF),
            pltpu.VMEM((4, 2, 64, TILE), BF),
            pltpu.VMEM((4, 2, 2, 64, TILE), BF),
            pltpu.VMEM((256, 1024), BF),
            pltpu.VMEM((LAGS, 256), F32),
            pltpu.VMEM((CHIPS, 16, TILE), BF),
            pltpu.VMEM((CHIPS, 16, TILE), BF),
            dma((4,)),
            dma(()),
            dma(()),
            dma((4,)),
            dma(()),
            dma((4,)),
            dma(()),
            dma((4,)),
            dma(()),
            dma((4,)),
        ],
        compiler_params=pltpu.CompilerParams(
            collective_id=0, has_side_effects=True, vmem_limit_bytes=48 << 20
        ),
    )(x, window_flags, pairs, held, table)
    return stacks + added[None]


def solution(mesh):
    in_specs = (
        P(None, None, "chan", "band"),
        P(),
        P("chan", None, None),
        P("chan", None, None),
        P("chan", "band", None, None),
    )
    out_specs = P("chan", "band", None, None)
    return jax.shard_map(body, mesh=mesh, in_specs=in_specs, out_specs=out_specs, check_vma=False)
```

```python
import math

import jax
import jax.numpy as jnp
import numpy as np
from jax import lax
from jax.experimental import pallas as pl
from jax.experimental.pallas import tpu as pltpu
from jax.sharding import PartitionSpec as P

TILE = 128
LAGS = 512
NF = 1024
NY, NZ = 4, 16
CHIPS = NY * NZ
QUARTERS = 4
TQ = 32
BINS = 8
FLOOR = 1e-05
BF = jnp.bfloat16
F32 = jnp.float32


def lag_table():
    tau = np.arange(LAGS) - LAGS // 2
    phase = np.mod(tau[:, None] * np.arange(NF)[None, :], NF)
    angles = phase.astype(np.float32) * np.float32(2.0 * math.pi / NF)
    amplitude = np.float32(1.0 / math.sqrt(NF))
    both = np.stack([np.cos(angles) * amplitude, -np.sin(angles) * amplitude])
    both = both.astype(np.float32).astype(jnp.bfloat16)
    both = both.reshape(2, LAGS, NY, NZ, 2, BINS)
    return both.transpose(2, 4, 1, 0, 3, 5).reshape(NY * 2, LAGS, 2 * NZ * BINS)


def place(tile, part):
    if tile < 8:
        return part * 8 + tile
    if tile < 24:
        return 32 + part * 16 + tile - 8
    return 96 + part * 8 + tile - 24


def send(src, dst, send_sem, recv_sem, where):
    pltpu.make_async_remote_copy(
        src_ref=src,
        dst_ref=dst,
        send_sem=send_sem,
        recv_sem=recv_sem,
        device_id=where,
        device_id_type=pl.DeviceIdType.MESH,
    ).start()


def wait_for(ref, sem):
    pltpu.make_async_copy(ref, ref, sem).wait()


def selection(quarter, core, fl_ref, pt_ref, ow_ref, s_mat):
    ii = lax.broadcasted_iota(jnp.int32, (TILE, TILE), 0)
    jj = lax.broadcasted_iota(jnp.int32, (TILE, TILE), 1)

    def row(values):
        return jnp.broadcast_to(values.astype(F32), (TILE, TILE))

    own = row(ow_ref[...])
    own_c = own.T
    rank = jnp.sum(jnp.where((own_c == own) & (jj < ii), 1.0, 0.0), axis=1, keepdims=True)
    holder = (2 * (jj % CHIPS) + core).astype(F32)
    order = (jj // CHIPS).astype(F32)
    chosen = jnp.where((own_c == holder) & (rank == order), 1.0, 0.0)
    a = jnp.sum(chosen * (row(pt_ref[0:1, :]).T + 1.0), axis=0, keepdims=True) - 1.0
    t = jnp.sum(chosen * (row(pt_ref[1:2, :]).T + 1.0), axis=0, keepdims=True) - 1.0
    tiles = ii.astype(F32)
    flags_a, flags_t = [], []
    for w in range(2):
        fc = row(fl_ref[w : w + 1, :]).T
        flags_a.append(jnp.sum(jnp.where(tiles == a, fc, 0.0), axis=0, keepdims=True))
        flags_t.append(jnp.sum(jnp.where(tiles == t, fc, 0.0), axis=0, keepdims=True))
    together = flags_a[0] * flags_t[0] + flags_a[1] * flags_t[1]
    share = jnp.where(together > 1.5, 0.5, 1.0)
    first = (quarter * TQ).astype(F32)
    a_here = a - first
    t_here = t - first
    low, mid = ii < 32, ii < 96
    part = jnp.where(low, ii // 8, jnp.where(mid, (ii - 32) // 16, (ii - 96) // 8))
    tile = jnp.where(low, ii % 8, jnp.where(mid, 8 + ii % 16, 24 + ii % 8)).astype(F32)
    edge_part = jnp.where(low, ii // 8, jnp.where(ii < 64, (ii - 32) // 8, -1))
    edge_tile = jnp.where(low, ii % 8 - 8, 32 + ii % 8).astype(F32)
    for p in range(4):
        w = p // 2
        left = pl.ds(p * TILE, TILE)
        right = pl.ds((4 + p) * TILE, TILE)
        here = part == p
        s_mat[0:TILE, left] = jnp.where(
            here & (tile == a_here), flags_a[w] * share, 0.0
        ).astype(BF)
        s_mat[0:TILE, right] = jnp.where(here & (tile == t_here), flags_t[w], 0.0).astype(BF)
        s_mat[TILE : 2 * TILE, left] = jnp.zeros((TILE, TILE), BF)
        s_mat[TILE : 2 * TILE, right] = jnp.where(
            (edge_part == p) & (edge_tile == t_here), flags_t[w], 0.0
        ).astype(BF)


def kernel(
    x_hbm, fl_hbm, pt_hbm, ow_hbm, w_hbm, out_ref,
    x_v, fl_v, pt_v, ow_v, w_v, a_f, b_f, b_h, r, hs, h, s_mat, acc, y_h, q_h,
    in_sems, w_sem, send1, recv1, sib_send, sib_recv, edge_send, edge_recv, send2, recv2,
):
    band = lax.axis_index("band")
    quarter = lax.axis_index("chan")
    chip, core = band // 2, band % 2
    y, z = chip // NZ, chip % NZ
    other = chip * 2 + 1 - core
    up = (quarter + 1) % QUARTERS
    down = (quarter + QUARTERS - 1) % QUARTERS

    loads = [
        pltpu.make_async_copy(x_hbm, x_v, in_sems.at[0]),
        pltpu.make_async_copy(fl_hbm, fl_v, in_sems.at[1]),
        pltpu.make_async_copy(pt_hbm, pt_v, in_sems.at[2]),
        pltpu.make_async_copy(ow_hbm, ow_v, in_sems.at[3]),
    ]
    for load in loads:
        load.start()
    load_w = pltpu.make_async_copy(w_hbm, w_v, w_sem)
    load_w.start()

    barrier = pltpu.get_barrier_semaphore()

    def greet(to_band, to_chan):
        pl.semaphore_signal(
            barrier, inc=1, device_id=(to_band, to_chan), device_id_type=pl.DeviceIdType.MESH
        )

    @pl.loop(1, CHIPS)
    def _(i):
        greet(((chip + i) % CHIPS) * 2 + core, quarter)

    greet(other, quarter)
    for beside in (up, down):
        greet(band, beside)
        greet(other, beside)

    for load in loads:
        load.wait()

    for tile in range(TQ):
        lanes = pl.ds(tile * TILE, TILE)
        for w in range(2):
            re = x_v[2 * w, :, lanes].astype(F32)
            im = x_v[2 * w + 1, :, lanes].astype(F32)
            energy = jnp.sum(re * re + im * im, axis=0, keepdims=True)
            scale = lax.rsqrt(energy * (1.0 / BINS) + FLOOR)
            a_f[pl.ds(8 * place(tile, 2 * w), 8), :] = re * scale
            a_f[pl.ds(8 * place(tile, 2 * w + 1), 8), :] = im * scale
    for i in range(BINS):
        b_f[pl.ds(i, TILE, stride=BINS), :] = a_f[pl.ds(i, TILE, stride=BINS), :].T
    b_h[...] = b_f[...].astype(BF).reshape(CHIPS, 16, TILE)

    pl.semaphore_wait(barrier, CHIPS - 1 + 5)

    def exchange(src, dst, send_sem, recv_sems):
        for t in (1, 2, 3, 0):
            row = (y + t) % NY

            @pl.loop(1 if t == 0 else 0, NZ)
            def _(i):
                g = row * NZ + (z + i) % NZ
                send(
                    src.at[g], dst.at[chip], send_sem, recv_sems.at[t],
                    (g * 2 + core, quarter),
                )

        pltpu.make_async_copy(src.at[chip], dst.at[chip], recv_sems.at[0]).start()

    exchange(b_h, r.at[0], send1, recv1)

    selection(quarter, core, fl_v, pt_v, ow_v, s_mat)
    acc[...] = jnp.zeros_like(acc)
    load_w.wait()

    block = lax.broadcasted_iota(jnp.int32, (64, TILE), 1) // 32

    def arrive(t):
        chips = pl.ds(((y + NY - t) % NY) * NZ, NZ)
        wait_for(r.at[0, chips], recv1.at[t])
        send(r.at[0, chips], r.at[1, chips], sib_send, sib_recv.at[t], (other, quarter))
        rows = r[0, chips].reshape(4, 64, TILE).astype(F32)
        high = rows[3]
        low = rows[0]
        for q in range(3):
            high = jnp.where(block == q, pltpu.roll(rows[q], (32 * q + 32) % TILE, 1), high)
        for q in range(1, 4):
            low = jnp.where(block == q, pltpu.roll(rows[q], 32 * q, 1), low)
        hs[t, 0] = high.astype(BF)
        hs[t, 1] = low.astype(BF)
        for d, beside in ((0, up), (1, down)):
            send(hs.at[t, d], h.at[t, 0, d], edge_send, edge_recv.at[t], (band, beside))
            send(hs.at[t, d], h.at[t, 1, d], edge_send, edge_recv.at[t], (other, beside))

    def compute(t):
        row = (y + NY - t) % NY
        chips = pl.ds(row * NZ, NZ)
        wait_for(h.at[t], edge_recv.at[t])
        wait_for(r.at[1, chips], sib_recv.at[t])
        total = None
        for o in range(2):
            from_low = h[t, o, 0].astype(F32)
            from_high = h[t, o, 1].astype(F32)
            edge = jnp.concatenate(
                [
                    jnp.where(
                        block == 0,
                        pltpu.roll(from_low, (TILE - 32 * q) % TILE, 1) if q else from_low,
                        pltpu.roll(from_high, (TILE + 32 - 32 * q) % TILE, 1)
                        if q != 1
                        else from_high,
                    )
                    for q in range(4)
                ],
                axis=0,
            ).astype(BF)
            rows = jnp.concatenate([r[o, chips].reshape(2 * TILE, TILE), edge], axis=1)
            g = jnp.dot(rows, s_mat[...], preferred_element_type=F32)
            left = [g[:, p * TILE : (p + 1) * TILE] for p in range(4)]
            right = [g[:, (4 + p) * TILE : (5 + p) * TILE] for p in range(4)]
            re = (left[0] * right[0] + left[1] * right[1]) + (
                left[2] * right[2] + left[3] * right[3]
            )
            im = (left[0] * right[1] - left[1] * right[0]) + (
                left[2] * right[3] - left[3] * right[2]
            )
            re = re.reshape(NZ, 2, BINS, TILE)
            im = im.reshape(NZ, 2, BINS, TILE)
            cross = jnp.concatenate(
                [
                    jnp.concatenate(
                        [v[:, k].reshape(TILE, TILE).astype(BF) for k in range(2)], axis=1
                    )
                    for v in (re, im)
                ],
                axis=0,
            )
            index = row * 2 + (core if o == 0 else 1 - core)
            part = jnp.dot(w_v[index], cross, preferred_element_type=F32)
            total = part if total is None else total + part
        acc[...] += total

    arrive(1)

    @pl.loop(2, 4)
    def _(t):
        arrive(t)
        compute(t - 1)

    arrive(0)
    compute(3)
    compute(0)

    for k in range(2):
        for c in range(4):
            turned = acc[c * TILE : (c + 1) * TILE, k * TILE : (k + 1) * TILE].T
            for s in range(2):
                b_f[pl.ds(k * 8 + s * 4 + c, CHIPS, stride=16), :] = turned[
                    s * CHIPS : (s + 1) * CHIPS
                ]
    y_h[...] = b_f[...].astype(BF).reshape(CHIPS, 16, TILE)
    exchange(y_h, q_h, send2, recv2)

    for t in (1, 2, 3, 0):
        row = (y + NY - t) % NY
        chips = pl.ds(row * NZ, NZ)
        wait_for(q_h.at[chips], recv2.at[t])
        a_f[pl.ds(row * 256, 256), :] = q_h[chips].astype(F32).reshape(256, TILE)
    for s in range(2):
        for c in range(4):
            out_ref[s, c * TILE : (c + 1) * TILE, :] = a_f[
                pl.ds(s * 4 + c, TILE, stride=BINS), :
            ].T

    most = pl.ds(0, CHIPS - 1)
    wait_for(b_h.at[most], send1)
    wait_for(y_h.at[most], send2)
    wait_for(r.at[0], sib_send)
    wait_for(h, edge_send)


def body(spectra, window_flags, pair_tiles, owners, stacks):
    x = jnp.transpose(spectra, (0, 1, 3, 2)).reshape(4, BINS, TQ * TILE)
    pairs = pair_tiles[0].T
    held = owners[0].T
    table = jnp.asarray(lag_table())
    dma = pltpu.SemaphoreType.DMA
    added = pl.pallas_call(
        kernel,
        out_shape=jax.ShapeDtypeStruct((2, LAGS, TILE), F32),
        in_specs=[pl.BlockSpec(memory_space=pltpu.HBM)] * 5,
        out_specs=pl.BlockSpec(memory_space=pltpu.VMEM),
        scratch_shapes=[
            pltpu.VMEM((4, BINS, TQ * TILE), BF),
            pltpu.VMEM((2, TILE), jnp.int32),
            pltpu.VMEM((2, TILE), jnp.int32),
            pltpu.VMEM((1, TILE), jnp.int32),
            pltpu.VMEM((NY * 2, LAGS, 256), BF),
            pltpu.VMEM((1024, TILE), F32),
            pltpu.VMEM((1024, TILE), F32),
            pltpu.VMEM((CHIPS, 16, TILE), BF),
            pltpu.VMEM((2, CHIPS, 16, TILE), BF),
            pltpu.VMEM((4, 2, 64, TILE), BF),
            pltpu.VMEM((4, 2, 2, 64, TILE), BF),
            pltpu.VMEM((256, 1024), BF),
            pltpu.VMEM((LAGS, 256), F32),
            pltpu.VMEM((CHIPS, 16, TILE), BF),
            pltpu.VMEM((CHIPS, 16, TILE), BF),
            dma((4,)),
            dma(()),
            dma(()),
            dma((4,)),
            dma(()),
            dma((4,)),
            dma(()),
            dma((4,)),
            dma(()),
            dma((4,)),
        ],
        compiler_params=pltpu.CompilerParams(
            collective_id=0, has_side_effects=True, vmem_limit_bytes=56 << 20
        ),
    )(x, window_flags, pairs, held, table)
    return stacks + added[None]


def solution(mesh):
    in_specs = (
        P(None, None, "chan", "band"),
        P(),
        P("chan", None, None),
        P("chan", None, None),
        P("chan", "band", None, None),
    )
    out_specs = P("chan", "band", None, None)
    return jax.shard_map(body, mesh=mesh, in_specs=in_specs, out_specs=out_specs, check_vma=False)
```

```python
import math

import jax
import jax.numpy as jnp
import numpy as np
from jax import lax
from jax.experimental import pallas as pl
from jax.experimental.pallas import tpu as pltpu
from jax.sharding import PartitionSpec as P

TILE = 128
LAGS = 512
NF = 1024
NY, NZ = 4, 16
CHIPS = NY * NZ
QUARTERS = 4
TQ = 32
BINS = 8
FLOOR = 1e-05
BF = jnp.bfloat16
F32 = jnp.float32


def lag_table():
    tau = np.arange(LAGS) - LAGS // 2
    phase = np.mod(tau[:, None] * np.arange(NF)[None, :], NF)
    angles = phase.astype(np.float32) * np.float32(2.0 * math.pi / NF)
    amplitude = np.float32(1.0 / math.sqrt(NF))
    both = np.stack([np.cos(angles) * amplitude, -np.sin(angles) * amplitude])
    both = both.astype(np.float32).astype(jnp.bfloat16)
    both = both.reshape(2, LAGS, NY, NZ * 2 * BINS)
    return both.transpose(2, 1, 0, 3).reshape(NY, LAGS, 4 * NZ * BINS)


def place(tile, part):
    if tile < 8:
        return part * 8 + tile
    if tile < 24:
        return 32 + part * 16 + tile - 8
    return 96 + part * 8 + tile - 24


def send(src, dst, send_sem, recv_sem, where):
    pltpu.make_async_remote_copy(
        src_ref=src,
        dst_ref=dst,
        send_sem=send_sem,
        recv_sem=recv_sem,
        device_id=where,
        device_id_type=pl.DeviceIdType.MESH,
    ).start()


def wait_for(ref, sem):
    pltpu.make_async_copy(ref, ref, sem).wait()


def selection(quarter, y, core, fl_ref, pt_ref, ow_ref, s_mat):
    ii = lax.broadcasted_iota(jnp.int32, (TILE, TILE), 0)
    jj = lax.broadcasted_iota(jnp.int32, (TILE, TILE), 1)

    def row(values):
        return jnp.broadcast_to(values.astype(F32), (TILE, TILE))

    own = row(ow_ref[...])
    own_c = own.T
    rank = jnp.sum(jnp.where((own_c == own) & (jj < ii), 1.0, 0.0), axis=1, keepdims=True)
    owner_y = (y + core + 2 * ((jj % 32) // NZ)) % NY
    holder = ((owner_y * NZ + jj % NZ) * 2 + jj // 64).astype(F32)
    order = ((jj // 32) % 2).astype(F32)
    chosen = jnp.where((own_c == holder) & (rank == order), 1.0, 0.0)
    a = jnp.sum(chosen * (row(pt_ref[0:1, :]).T + 1.0), axis=0, keepdims=True) - 1.0
    t = jnp.sum(chosen * (row(pt_ref[1:2, :]).T + 1.0), axis=0, keepdims=True) - 1.0
    tiles = ii.astype(F32)
    flags_a, flags_t = [], []
    for w in range(2):
        fc = row(fl_ref[w : w + 1, :]).T
        flags_a.append(jnp.sum(jnp.where(tiles == a, fc, 0.0), axis=0, keepdims=True))
        flags_t.append(jnp.sum(jnp.where(tiles == t, fc, 0.0), axis=0, keepdims=True))
    together = flags_a[0] * flags_t[0] + flags_a[1] * flags_t[1]
    share = jnp.where(together > 1.5, 0.5, 1.0)
    first = (quarter * TQ).astype(F32)
    a_here = a - first
    t_here = t - first
    low, mid = ii < 32, ii < 96
    part = jnp.where(low, ii // 8, jnp.where(mid, (ii - 32) // 16, (ii - 96) // 8))
    tile = jnp.where(low, ii % 8, jnp.where(mid, 8 + ii % 16, 24 + ii % 8)).astype(F32)
    edge_part = jnp.where(low, ii // 8, jnp.where(ii < 64, (ii - 32) // 8, -1))
    edge_tile = jnp.where(low, ii % 8 - 8, 32 + ii % 8).astype(F32)
    for p in range(4):
        w = p // 2
        left = pl.ds(p * TILE, TILE)
        right = pl.ds((4 + p) * TILE, TILE)
        here = part == p
        s_mat[0:TILE, left] = jnp.where(
            here & (tile == a_here), flags_a[w] * share, 0.0
        ).astype(BF)
        s_mat[0:TILE, right] = jnp.where(here & (tile == t_here), flags_t[w], 0.0).astype(BF)
        s_mat[TILE : 2 * TILE, left] = jnp.zeros((TILE, TILE), BF)
        s_mat[TILE : 2 * TILE, right] = jnp.where(
            (edge_part == p) & (edge_tile == t_here), flags_t[w], 0.0
        ).astype(BF)


def kernel(
    x_hbm, fl_hbm, pt_hbm, ow_hbm, w_hbm, out_ref,
    x_v, fl_v, pt_v, ow_v, w_v, a_f, b_f, b_k, x_in, m, r, hs, h, s_mat, acc, y_f, y_h, q_h, ps, pr,
    in_sems, w_sem, pre_send, pre_recv, send1, recv1, sib_send, sib_recv, edge_send, edge_recv,
    send2, recv2, post_send, post_recv,
):
    band = lax.axis_index("band")
    quarter = lax.axis_index("chan")
    chip, core = band // 2, band % 2
    y, z = chip // NZ, chip % NZ
    other = chip * 2 + 1 - core
    up, down = quarter + 1, quarter - 1
    has_up, has_down = quarter < QUARTERS - 1, quarter > 0

    barrier = pltpu.get_barrier_semaphore()

    def greet(to_band, to_chan):
        pl.semaphore_signal(
            barrier, inc=1, device_id=(to_band, to_chan), device_id_type=pl.DeviceIdType.MESH
        )

    def row_of(who, j):
        return (y + who + 2 * j) % NY

    def step(i):
        return jnp.where(i % 2 == 1, NZ // 2 - (i + 1) // 2, NZ // 2 + i // 2)

    loads = [
        pltpu.make_async_copy(x_hbm, x_v, in_sems.at[0]),
        pltpu.make_async_copy(fl_hbm, fl_v, in_sems.at[1]),
        pltpu.make_async_copy(pt_hbm, pt_v, in_sems.at[2]),
        pltpu.make_async_copy(ow_hbm, ow_v, in_sems.at[3]),
    ]
    for load in loads:
        load.start()
    load_w = pltpu.make_async_copy(w_hbm, w_v, w_sem)
    load_w.start()

    @pl.loop(0, NZ)
    def _(i):
        for j in range(2):
            g = row_of(core, j) * NZ + (z + step(i)) % NZ

            @pl.when(g != chip)
            def _():
                greet(g * 2 + core, quarter)

    greet(other, quarter)
    for there, beside in ((has_up, up), (has_down, down)):

        @pl.when(there)
        def _():
            greet(band, beside)
            greet(other, beside)

    for load in loads:
        load.wait()

    for tile in range(TQ):
        lanes = pl.ds(tile * TILE, TILE)
        for w in range(2):
            re = x_v[2 * w, :, lanes].astype(F32)
            im = x_v[2 * w + 1, :, lanes].astype(F32)
            energy = jnp.sum(re * re + im * im, axis=0, keepdims=True)
            scale = lax.rsqrt(energy * (1.0 / BINS) + FLOOR)
            a_f[pl.ds(8 * place(tile, 2 * w), 8), :] = re * scale
            a_f[pl.ds(8 * place(tile, 2 * w + 1), 8), :] = im * scale
    for i in range(BINS):
        b_f[pl.ds(i, TILE, stride=BINS), :] = a_f[pl.ds(i, TILE, stride=BINS), :].T
    for b in range(2):
        b_k[b] = (
            b_f[...].reshape(CHIPS, 2, BINS, TILE)[:, b].reshape(NY, 8, 16, TILE).astype(BF)
        )

    pl.semaphore_wait(
        barrier, 32 + core + 2 * has_up.astype(jnp.int32) + 2 * has_down.astype(jnp.int32)
    )

    for b in range(2):
        for j in range(2):
            send(
                b_k.at[b, row_of(1 - core, j)], x_in.at[b, j], pre_send, pre_recv.at[b],
                (other, quarter),
            )

    def merge(b):
        wait_for(x_in.at[b], pre_recv.at[b])
        for j in range(2):
            rows = b_f[pl.ds(row_of(core, j) * 256, 256), :]
            own = rows.reshape(NZ, 2, BINS, TILE)[:, b]
            theirs = x_in[b, j].astype(F32).reshape(NZ, BINS, TILE)
            low = jnp.where(core == 0, own, theirs)
            high = jnp.where(core == 0, theirs, own)
            both = jnp.stack([low, high], axis=1)
            m[b, j] = both.reshape(NZ, 16, TILE).astype(BF)

    def dispatch(src, dst, b, j, send_sem, recv_sem):
        to_y = row_of(core, j)
        there = (j + core) % 2

        @pl.loop(0, NZ)
        def _(i):
            to_z = (z + step(i)) % NZ
            g = to_y * NZ + to_z

            @pl.when(g != chip)
            def _():
                send(
                    src.at[b, j, to_z], dst.at[2 * b + there, z], send_sem, recv_sem(there),
                    (g * 2 + core, quarter),
                )

        if j == 0:

            @pl.when(core == 0)
            def _():
                pltpu.make_async_copy(src.at[b, 0, z], dst.at[2 * b, z], recv_sem(0)).start()

    def left(src, b, j, send_sem):
        wait_for(src.at[b, j, pl.ds(0, NZ - 1)], send_sem)
        if j == 0:

            @pl.when(core == 1)
            def _():
                wait_for(src.at[b, j, 0], send_sem)

        else:
            wait_for(src.at[b, j, 0], send_sem)

    merge(0)
    for j in range(2):
        dispatch(m, r.at[0], 0, j, send1.at[j], lambda there: recv1.at[there])
    merge(1)
    selection(quarter, y, core, fl_v, pt_v, ow_v, s_mat)
    acc[...] = jnp.zeros_like(acc)
    for d, there in ((0, has_down), (1, has_up)):

        @pl.when(jnp.logical_not(there))
        def _():
            h[:, d] = jnp.zeros((4, 2, 64, TILE), BF)

    for j in range(2):
        left(m, 0, j, send1.at[j])
        dispatch(m, r.at[0], 1, j, send1.at[2 + j], lambda there: recv1.at[2 + there])
    load_w.wait()

    block = lax.broadcasted_iota(jnp.int32, (64, TILE), 1) // 32

    def arrive(t):
        wait_for(r.at[0, t], recv1.at[t])
        send(r.at[0, t], r.at[1, t], sib_send, sib_recv.at[t], (other, quarter))
        rows = r[0, t].reshape(4, 64, TILE).astype(F32)
        high = rows[3]
        low = rows[0]
        for q in range(3):
            high = jnp.where(block == q, pltpu.roll(rows[q], (32 * q + 32) % TILE, 1), high)
        for q in range(1, 4):
            low = jnp.where(block == q, pltpu.roll(rows[q], 32 * q, 1), low)
        hs[t, 0] = high.astype(BF)
        hs[t, 1] = low.astype(BF)
        for d, there, beside in ((0, has_up, up), (1, has_down, down)):

            @pl.when(there)
            def _():
                send(hs.at[t, d], h.at[t, d, 0], edge_send.at[d], edge_recv.at[t, d], (band, beside))
                send(hs.at[t, d], h.at[t, d, 1], edge_send.at[d], edge_recv.at[t, d], (other, beside))

    def compute(t):
        for d, there in ((0, has_down), (1, has_up)):

            @pl.when(there)
            def _():
                wait_for(h.at[t, d], edge_recv.at[t, d])

        wait_for(r.at[1, t], sib_recv.at[t])
        total = None
        for o in range(2):
            from_low = h[t, 0, o].astype(F32)
            from_high = h[t, 1, o].astype(F32)
            edge = jnp.concatenate(
                [
                    jnp.where(
                        block == 0,
                        pltpu.roll(from_low, (TILE - 32 * q) % TILE, 1) if q else from_low,
                        pltpu.roll(from_high, (TILE + 32 - 32 * q) % TILE, 1)
                        if q != 1
                        else from_high,
                    )
                    for q in range(4)
                ],
                axis=0,
            ).astype(BF)
            rows = jnp.concatenate([r[o, t].reshape(2 * TILE, TILE), edge], axis=1)
            g = jnp.dot(rows, s_mat[...], preferred_element_type=F32)
            left = [g[:, p * TILE : (p + 1) * TILE] for p in range(4)]
            right = [g[:, (4 + p) * TILE : (5 + p) * TILE] for p in range(4)]
            re = (left[0] * right[0] + left[1] * right[1]) + (
                left[2] * right[2] + left[3] * right[3]
            )
            im = (left[0] * right[1] - left[1] * right[0]) + (
                left[2] * right[3] - left[3] * right[2]
            )
            cross = jnp.concatenate([re, im], axis=0).astype(BF)
            index = row_of(core if o == 0 else 1 - core, t % 2)
            part = jnp.dot(w_v[index], cross, preferred_element_type=F32)
            total = part if total is None else total + part
        acc[t // 2] += total

    def finish(b):
        for c in range(4):
            turned = acc[b, c * TILE : (c + 1) * TILE, :].T
            for s in range(4):
                y_f[pl.ds(s * 4 + c, 32, stride=16), :] = turned[s * 32 : (s + 1) * 32]
        y_h[b] = y_f[...].astype(BF).reshape(2, NZ, 16, TILE)
        for j in range(2):
            dispatch(y_h, q_h, b, j, send2.at[b, j], lambda there: recv2.at[b])

    def put(values, b, who):
        for j in range(2):
            first = row_of(who, j) * 256 + b * 8
            for i in range(NZ):
                a_f[pl.ds(pl.multiple_of(first + i * 16, 8), 8), :] = values[j, i]

    def collect(b):
        halves = pl.ds(2 * b, 2)
        wait_for(q_h.at[halves], recv2.at[b])
        got = q_h[halves].astype(F32).reshape(2, NZ, 2, 8, TILE)
        theirs = jnp.where(core == 0, got[:, :, 1], got[:, :, 0])
        ps[b] = theirs.reshape(2, 8, 16, TILE).astype(BF)
        send(ps.at[b], pr.at[b], post_send, post_recv.at[b], (other, quarter))
        put(jnp.where(core == 0, got[:, :, 0], got[:, :, 1]), b, core)

    def join(b):
        wait_for(pr.at[b], post_recv.at[b])
        put(pr[b].astype(F32).reshape(2, NZ, 8, TILE), b, 1 - core)

    arrive(0)
    arrive(1)
    compute(0)
    compute(1)
    finish(0)
    arrive(2)
    arrive(3)
    compute(2)
    compute(3)
    finish(1)
    collect(0)
    join(0)
    collect(1)
    join(1)
    for s in range(2):
        for c in range(4):
            out_ref[s, c * TILE : (c + 1) * TILE, :] = a_f[
                pl.ds(s * 4 + c, TILE, stride=BINS), :
            ].T

    for j in range(2):
        left(m, 1, j, send1.at[2 + j])
        for b in range(2):
            left(y_h, b, j, send2.at[b, j])
    wait_for(x_in, pre_send)
    wait_for(r.at[0], sib_send)
    wait_for(ps, post_send)
    for d, there in ((0, has_up), (1, has_down)):

        @pl.when(there)
        def _():
            wait_for(h.at[:, d], edge_send.at[d])


def body(spectra, window_flags, pair_tiles, owners, stacks):
    x = jnp.transpose(spectra, (0, 1, 3, 2)).reshape(4, BINS, TQ * TILE)
    pairs = pair_tiles[0].T
    held = owners[0].T
    table = jnp.asarray(lag_table())
    dma = pltpu.SemaphoreType.DMA
    added = pl.pallas_call(
        kernel,
        out_shape=jax.ShapeDtypeStruct((2, LAGS, TILE), F32),
        in_specs=[pl.BlockSpec(memory_space=pltpu.HBM)] * 5,
        out_specs=pl.BlockSpec(memory_space=pltpu.VMEM),
        scratch_shapes=[
            pltpu.VMEM((4, BINS, TQ * TILE), BF),
            pltpu.VMEM((2, TILE), jnp.int32),
            pltpu.VMEM((2, TILE), jnp.int32),
            pltpu.VMEM((1, TILE), jnp.int32),
            pltpu.VMEM((NY, LAGS, 512), BF),
            pltpu.VMEM((1024, TILE), F32),
            pltpu.VMEM((1024, TILE), F32),
            pltpu.VMEM((2, NY, 8, 16, TILE), BF),
            pltpu.VMEM((2, 2, 8, 16, TILE), BF),
            pltpu.VMEM((2, 2, NZ, 16, TILE), BF),
            pltpu.VMEM((2, 4, NZ, 16, TILE), BF),
            pltpu.VMEM((4, 2, 64, TILE), BF),
            pltpu.VMEM((4, 2, 2, 64, TILE), BF),
            pltpu.VMEM((256, 1024), BF),
            pltpu.VMEM((2, LAGS, TILE), F32),
            pltpu.VMEM((512, TILE), F32),
            pltpu.VMEM((2, 2, NZ, 16, TILE), BF),
            pltpu.VMEM((4, NZ, 16, TILE), BF),
            pltpu.VMEM((2, 2, 8, 16, TILE), BF),
            pltpu.VMEM((2, 2, 8, 16, TILE), BF),
            dma((4,)),
            dma(()),
            dma(()),
            dma((2,)),
            dma((4,)),
            dma((4,)),
            dma(()),
            dma((4,)),
            dma((2,)),
            dma((4, 2)),
            dma((2, 2)),
            dma((2,)),
            dma(()),
            dma((2,)),
        ],
        compiler_params=pltpu.CompilerParams(
            collective_id=0, has_side_effects=True, vmem_limit_bytes=56 << 20
        ),
    )(x, window_flags, pairs, held, table)
    return stacks + added[None]


def solution(mesh):
    in_specs = (
        P(None, None, "chan", "band"),
        P(),
        P("chan", None, None),
        P("chan", None, None),
        P("chan", "band", None, None),
    )
    out_specs = P("chan", "band", None, None)
    return jax.shard_map(body, mesh=mesh, in_specs=in_specs, out_specs=out_specs, check_vma=False)
```

```python
import math

import jax
import jax.numpy as jnp
import numpy as np
from jax import lax
from jax.experimental import pallas as pl
from jax.experimental.pallas import tpu as pltpu
from jax.sharding import PartitionSpec as P

TILE = 128
LAGS = 512
NF = 1024
NY, NZ = 4, 16
CHIPS = NY * NZ
QUARTERS = 4
TQ = 32
BINS = 8
FLOOR = 1e-05
BF = jnp.bfloat16
F32 = jnp.float32


def lag_table():
    tau = np.arange(LAGS) - LAGS // 2
    phase = np.mod(tau[:, None] * np.arange(NF)[None, :], NF)
    angles = phase.astype(np.float32) * np.float32(2.0 * math.pi / NF)
    amplitude = np.float32(1.0 / math.sqrt(NF))
    both = np.stack([np.cos(angles) * amplitude, -np.sin(angles) * amplitude])
    both = both.astype(np.float32).astype(jnp.bfloat16)
    both = both.reshape(2, LAGS, NY, NZ * 2 * BINS)
    return both.transpose(2, 1, 0, 3).reshape(NY, LAGS, 4 * NZ * BINS)


def place(tile, part):
    if tile < 8:
        return part * 8 + tile
    if tile < 24:
        return 32 + part * 16 + tile - 8
    return 96 + part * 8 + tile - 24


def send(src, dst, send_sem, recv_sem, where):
    pltpu.make_async_remote_copy(
        src_ref=src,
        dst_ref=dst,
        send_sem=send_sem,
        recv_sem=recv_sem,
        device_id=where,
        device_id_type=pl.DeviceIdType.MESH,
    ).start()


def wait_for(ref, sem):
    pltpu.make_async_copy(ref, ref, sem).wait()


def selection(quarter, y, core, fl_ref, pt_ref, ow_ref, s_mat):
    ii = lax.broadcasted_iota(jnp.int32, (TILE, TILE), 0)
    jj = lax.broadcasted_iota(jnp.int32, (TILE, TILE), 1)

    def row(values):
        return jnp.broadcast_to(values.astype(F32), (TILE, TILE))

    own = row(ow_ref[...])
    own_c = own.T
    rank = jnp.sum(jnp.where((own_c == own) & (jj < ii), 1.0, 0.0), axis=1, keepdims=True)
    owner_y = (y + core + 2 * ((jj % 32) // NZ)) % NY
    holder = ((owner_y * NZ + jj % NZ) * 2 + jj // 64).astype(F32)
    order = ((jj // 32) % 2).astype(F32)
    chosen = jnp.where((own_c == holder) & (rank == order), 1.0, 0.0)
    a = jnp.sum(chosen * (row(pt_ref[0:1, :]).T + 1.0), axis=0, keepdims=True) - 1.0
    t = jnp.sum(chosen * (row(pt_ref[1:2, :]).T + 1.0), axis=0, keepdims=True) - 1.0
    tiles = ii.astype(F32)
    flags_a, flags_t = [], []
    for w in range(2):
        fc = row(fl_ref[w : w + 1, :]).T
        flags_a.append(jnp.sum(jnp.where(tiles == a, fc, 0.0), axis=0, keepdims=True))
        flags_t.append(jnp.sum(jnp.where(tiles == t, fc, 0.0), axis=0, keepdims=True))
    together = flags_a[0] * flags_t[0] + flags_a[1] * flags_t[1]
    share = jnp.where(together > 1.5, 0.5, 1.0)
    first = (quarter * TQ).astype(F32)
    a_here = a - first
    t_here = t - first
    low, mid = ii < 32, ii < 96
    part = jnp.where(low, ii // 8, jnp.where(mid, (ii - 32) // 16, (ii - 96) // 8))
    tile = jnp.where(low, ii % 8, jnp.where(mid, 8 + ii % 16, 24 + ii % 8)).astype(F32)
    edge_part = jnp.where(low, ii // 8, jnp.where(ii < 64, (ii - 32) // 8, -1))
    edge_tile = jnp.where(low, ii % 8 - 8, 32 + ii % 8).astype(F32)
    for p in range(4):
        w = p // 2
        left = pl.ds(p * TILE, TILE)
        right = pl.ds((4 + p) * TILE, TILE)
        here = part == p
        s_mat[0:TILE, left] = jnp.where(
            here & (tile == a_here), flags_a[w] * share, 0.0
        ).astype(BF)
        s_mat[0:TILE, right] = jnp.where(here & (tile == t_here), flags_t[w], 0.0).astype(BF)
        s_mat[TILE : 2 * TILE, left] = jnp.zeros((TILE, TILE), BF)
        s_mat[TILE : 2 * TILE, right] = jnp.where(
            (edge_part == p) & (edge_tile == t_here), flags_t[w], 0.0
        ).astype(BF)


def kernel(
    x_hbm, fl_hbm, pt_hbm, ow_hbm, w_hbm, out_ref,
    x_v, fl_v, pt_v, ow_v, w_v, a_f, b_f, b_k, x_in, m, r, hs, h, s_mat, acc, y_f, y_h, q_h, ps, pr,
    in_sems, w_sem, pre_send, pre_recv, send1, recv1, sib_send, sib_recv, edge_send, edge_recv,
    send2, recv2, post_send, post_recv,
):
    band = lax.axis_index("band")
    quarter = lax.axis_index("chan")
    chip, core = band // 2, band % 2
    y, z = chip // NZ, chip % NZ
    other = chip * 2 + 1 - core
    up, down = quarter + 1, quarter - 1
    has_up, has_down = quarter < QUARTERS - 1, quarter > 0

    barrier = pltpu.get_barrier_semaphore()

    def greet(to_band, to_chan):
        pl.semaphore_signal(
            barrier, inc=1, device_id=(to_band, to_chan), device_id_type=pl.DeviceIdType.MESH
        )

    def row_of(who, j):
        return (y + who + 2 * j) % NY

    def step(i):
        return jnp.where(i % 2 == 1, NZ // 2 - (i + 1) // 2, NZ // 2 + i // 2)

    loads = [
        pltpu.make_async_copy(x_hbm, x_v, in_sems.at[0]),
        pltpu.make_async_copy(fl_hbm, fl_v, in_sems.at[1]),
        pltpu.make_async_copy(pt_hbm, pt_v, in_sems.at[2]),
        pltpu.make_async_copy(ow_hbm, ow_v, in_sems.at[3]),
    ]
    for load in loads:
        load.start()
    load_w = pltpu.make_async_copy(w_hbm, w_v, w_sem)
    load_w.start()

    @pl.loop(0, NZ)
    def _(i):
        for j in range(2):
            g = row_of(core, j) * NZ + (z + step(i)) % NZ

            @pl.when(g != chip)
            def _():
                greet(g * 2 + core, quarter)

    greet(other, quarter)
    for there, beside in ((has_up, up), (has_down, down)):

        @pl.when(there)
        def _():
            greet(band, beside)
            greet(other, beside)

    for load in loads:
        load.wait()

    for tile in range(TQ):
        lanes = pl.ds(tile * TILE, TILE)
        for w in range(2):
            re = x_v[2 * w, :, lanes].astype(F32)
            im = x_v[2 * w + 1, :, lanes].astype(F32)
            energy = jnp.sum(re * re + im * im, axis=0, keepdims=True)
            scale = lax.rsqrt(energy * (1.0 / BINS) + FLOOR)
            a_f[pl.ds(8 * place(tile, 2 * w), 8), :] = re * scale
            a_f[pl.ds(8 * place(tile, 2 * w + 1), 8), :] = im * scale
    for i in range(BINS):
        b_f[pl.ds(i, TILE, stride=BINS), :] = a_f[pl.ds(i, TILE, stride=BINS), :].T
    for b in range(2):
        b_k[b] = (
            b_f[...].reshape(CHIPS, 2, BINS, TILE)[:, b].reshape(NY, 8, 16, TILE).astype(BF)
        )

    pl.semaphore_wait(
        barrier, 32 + core + 2 * has_up.astype(jnp.int32) + 2 * has_down.astype(jnp.int32)
    )

    for b in range(2):
        for j in range(2):
            send(
                b_k.at[b, row_of(1 - core, j)], x_in.at[b, j], pre_send, pre_recv.at[b],
                (other, quarter),
            )

    def merge(b):
        wait_for(x_in.at[b], pre_recv.at[b])
        for j in range(2):
            rows = b_f[pl.ds(row_of(core, j) * 256, 256), :]
            own = rows.reshape(NZ, 2, BINS, TILE)[:, b]
            theirs = x_in[b, j].astype(F32).reshape(NZ, BINS, TILE)
            low = jnp.where(core == 0, own, theirs)
            high = jnp.where(core == 0, theirs, own)
            both = jnp.stack([low, high], axis=1)
            m[b, j] = both.reshape(NZ, 16, TILE).astype(BF)

    def dispatch(src, dst, b, j, send_sem, recv_sem):
        to_y = row_of(core, j)
        there = (j + core) % 2

        @pl.loop(0, NZ)
        def _(i):
            to_z = (z + step(i)) % NZ
            g = to_y * NZ + to_z

            @pl.when(g != chip)
            def _():
                send(
                    src.at[b, j, to_z], dst.at[2 * b + there, z], send_sem, recv_sem(there),
                    (g * 2 + core, quarter),
                )

        if j == 0:

            @pl.when(core == 0)
            def _():
                pltpu.make_async_copy(src.at[b, 0, z], dst.at[2 * b, z], recv_sem(0)).start()

    def left(src, b, j, send_sem):
        wait_for(src.at[b, j, pl.ds(0, NZ - 1)], send_sem)
        if j == 0:

            @pl.when(core == 1)
            def _():
                wait_for(src.at[b, j, 0], send_sem)

        else:
            wait_for(src.at[b, j, 0], send_sem)

    merge(0)
    for j in range(2):
        dispatch(m, r.at[0], 0, j, send1.at[j], lambda there: recv1.at[there])
    merge(1)
    selection(quarter, y, core, fl_v, pt_v, ow_v, s_mat)
    acc[...] = jnp.zeros_like(acc)
    for d, there in ((0, has_down), (1, has_up)):

        @pl.when(jnp.logical_not(there))
        def _():
            h[:, d] = jnp.zeros((4, 2, 64, TILE), BF)

    for j in range(2):
        left(m, 0, j, send1.at[j])
        dispatch(m, r.at[0], 1, j, send1.at[2 + j], lambda there: recv1.at[2 + there])
    load_w.wait()

    block = lax.broadcasted_iota(jnp.int32, (64, TILE), 1) // 32

    def arrive(t):
        wait_for(r.at[0, t], recv1.at[t])
        send(r.at[0, t], r.at[1, t], sib_send, sib_recv.at[t], (other, quarter))
        rows = r[0, t].reshape(4, 64, TILE).astype(F32)
        high = rows[3]
        low = rows[0]
        for q in range(3):
            high = jnp.where(block == q, pltpu.roll(rows[q], (32 * q + 32) % TILE, 1), high)
        for q in range(1, 4):
            low = jnp.where(block == q, pltpu.roll(rows[q], 32 * q, 1), low)
        hs[t, 0] = high.astype(BF)
        hs[t, 1] = low.astype(BF)
        for d, there, beside in ((0, has_up, up), (1, has_down, down)):

            @pl.when(there)
            def _():
                send(hs.at[t, d], h.at[t, d, 0], edge_send.at[d], edge_recv.at[t, d], (band, beside))
                send(hs.at[t, d], h.at[t, d, 1], edge_send.at[d], edge_recv.at[t, d], (other, beside))

    def compute(t):
        for d, there in ((0, has_down), (1, has_up)):

            @pl.when(there)
            def _():
                wait_for(h.at[t, d], edge_recv.at[t, d])

        wait_for(r.at[1, t], sib_recv.at[t])
        total = None
        for o in range(2):
            from_low = h[t, 0, o].astype(F32)
            from_high = h[t, 1, o].astype(F32)
            edge = jnp.concatenate(
                [
                    jnp.where(
                        block == 0,
                        pltpu.roll(from_low, (TILE - 32 * q) % TILE, 1) if q else from_low,
                        pltpu.roll(from_high, (TILE + 32 - 32 * q) % TILE, 1)
                        if q != 1
                        else from_high,
                    )
                    for q in range(4)
                ],
                axis=0,
            ).astype(BF)
            rows = jnp.concatenate([r[o, t].reshape(2 * TILE, TILE), edge], axis=1)
            g = jnp.dot(rows, s_mat[...], preferred_element_type=F32)
            left = [g[:, p * TILE : (p + 1) * TILE] for p in range(4)]
            right = [g[:, (4 + p) * TILE : (5 + p) * TILE] for p in range(4)]
            re = (left[0] * right[0] + left[1] * right[1]) + (
                left[2] * right[2] + left[3] * right[3]
            )
            im = (left[0] * right[1] - left[1] * right[0]) + (
                left[2] * right[3] - left[3] * right[2]
            )
            cross = jnp.concatenate([re, im], axis=0).astype(BF)
            index = row_of(core if o == 0 else 1 - core, t % 2)
            part = jnp.dot(w_v[index], cross, preferred_element_type=F32)
            total = part if total is None else total + part
        acc[t // 2] += total

    def finish(b):
        for c in range(4):
            turned = acc[b, c * TILE : (c + 1) * TILE, :].T
            for s in range(4):
                y_f[pl.ds(s * 4 + c, 32, stride=16), :] = turned[s * 32 : (s + 1) * 32]
        y_h[b] = y_f[...].astype(BF).reshape(2, NZ, 16, TILE)
        for j in range(2):
            dispatch(y_h, q_h, b, j, send2.at[b, j], lambda there: recv2.at[2 * b + there])

    def put(values, t, who):
        first = row_of(who, t % 2) * 256 + t // 2 * 8
        for i in range(NZ):
            a_f[pl.ds(pl.multiple_of(first + i * 16, 8), 8), :] = values[i]

    def collect(t):
        wait_for(q_h.at[t], recv2.at[t])
        got = q_h[t].astype(F32).reshape(NZ, 2, 8, TILE)
        theirs = jnp.where(core == 0, got[:, 1], got[:, 0])
        ps[t] = theirs.reshape(8, 16, TILE).astype(BF)
        send(ps.at[t], pr.at[t], post_send, post_recv.at[t], (other, quarter))
        put(jnp.where(core == 0, got[:, 0], got[:, 1]), t, core)

    def join(t):
        wait_for(pr.at[t], post_recv.at[t])
        put(pr[t].astype(F32).reshape(NZ, 8, TILE), t, 1 - core)

    arrive(0)
    arrive(1)
    compute(0)
    compute(1)
    finish(0)
    arrive(2)
    arrive(3)
    compute(2)
    compute(3)
    finish(1)
    for t in range(4):
        collect(t)
        if t >= 1:
            join(t - 1)
    join(3)
    for s in range(2):
        for c in range(4):
            out_ref[s, c * TILE : (c + 1) * TILE, :] = a_f[
                pl.ds(s * 4 + c, TILE, stride=BINS), :
            ].T

    for j in range(2):
        left(m, 1, j, send1.at[2 + j])
        for b in range(2):
            left(y_h, b, j, send2.at[b, j])
    wait_for(x_in, pre_send)
    wait_for(r.at[0], sib_send)
    wait_for(ps, post_send)
    for d, there in ((0, has_up), (1, has_down)):

        @pl.when(there)
        def _():
            wait_for(h.at[:, d], edge_send.at[d])


def body(spectra, window_flags, pair_tiles, owners, stacks):
    x = jnp.transpose(spectra, (0, 1, 3, 2)).reshape(4, BINS, TQ * TILE)
    pairs = pair_tiles[0].T
    held = owners[0].T
    table = jnp.asarray(lag_table())
    dma = pltpu.SemaphoreType.DMA
    added = pl.pallas_call(
        kernel,
        out_shape=jax.ShapeDtypeStruct((2, LAGS, TILE), F32),
        in_specs=[pl.BlockSpec(memory_space=pltpu.HBM)] * 5,
        out_specs=pl.BlockSpec(memory_space=pltpu.VMEM),
        scratch_shapes=[
            pltpu.VMEM((4, BINS, TQ * TILE), BF),
            pltpu.VMEM((2, TILE), jnp.int32),
            pltpu.VMEM((2, TILE), jnp.int32),
            pltpu.VMEM((1, TILE), jnp.int32),
            pltpu.VMEM((NY, LAGS, 512), BF),
            pltpu.VMEM((1024, TILE), F32),
            pltpu.VMEM((1024, TILE), F32),
            pltpu.VMEM((2, NY, 8, 16, TILE), BF),
            pltpu.VMEM((2, 2, 8, 16, TILE), BF),
            pltpu.VMEM((2, 2, NZ, 16, TILE), BF),
            pltpu.VMEM((2, 4, NZ, 16, TILE), BF),
            pltpu.VMEM((4, 2, 64, TILE), BF),
            pltpu.VMEM((4, 2, 2, 64, TILE), BF),
            pltpu.VMEM((256, 1024), BF),
            pltpu.VMEM((2, LAGS, TILE), F32),
            pltpu.VMEM((512, TILE), F32),
            pltpu.VMEM((2, 2, NZ, 16, TILE), BF),
            pltpu.VMEM((4, NZ, 16, TILE), BF),
            pltpu.VMEM((4, 8, 16, TILE), BF),
            pltpu.VMEM((4, 8, 16, TILE), BF),
            dma((4,)),
            dma(()),
            dma(()),
            dma((2,)),
            dma((4,)),
            dma((4,)),
            dma(()),
            dma((4,)),
            dma((2,)),
            dma((4, 2)),
            dma((2, 2)),
            dma((4,)),
            dma(()),
            dma((4,)),
        ],
        compiler_params=pltpu.CompilerParams(
            collective_id=0, has_side_effects=True, vmem_limit_bytes=32 << 20
        ),
    )(
        *(
            pltpu.with_memory_space_constraint(v, pltpu.HBM)
            for v in (x, window_flags, pairs, held, table)
        )
    )
    return stacks + added[None]


def solution(mesh):
    in_specs = (
        P(None, None, "chan", "band"),
        P(),
        P("chan", None, None),
        P("chan", None, None),
        P("chan", "band", None, None),
    )
    out_specs = P("chan", "band", None, None)
    return jax.shard_map(body, mesh=mesh, in_specs=in_specs, out_specs=out_specs, check_vma=False)
```

```python
import math

import jax
import jax.numpy as jnp
import numpy as np
from jax import lax
from jax.experimental import pallas as pl
from jax.experimental.pallas import tpu as pltpu
from jax.sharding import PartitionSpec as P

TILE = 128
LAGS = 512
NF = 1024
NY, NZ = 4, 16
CHIPS = NY * NZ
QUARTERS = 4
TQ = 32
BINS = 8
FLOOR = 1e-05
BF = jnp.bfloat16
F32 = jnp.float32


def lag_table():
    tau = np.arange(LAGS) - LAGS // 2
    phase = np.mod(tau[:, None] * np.arange(NF)[None, :], NF)
    angles = phase.astype(np.float32) * np.float32(2.0 * math.pi / NF)
    amplitude = np.float32(1.0 / math.sqrt(NF))
    both = np.stack([np.cos(angles) * amplitude, -np.sin(angles) * amplitude])
    both = both.astype(np.float32).astype(jnp.bfloat16)
    both = both.reshape(2, LAGS, NY, NZ * 2 * BINS)
    return both.transpose(2, 1, 0, 3).reshape(NY, LAGS, 4 * NZ * BINS)


def place(tile, part):
    if tile < 8:
        return part * 8 + tile
    if tile < 24:
        return 32 + part * 16 + tile - 8
    return 96 + part * 8 + tile - 24


def send(src, dst, send_sem, recv_sem, where):
    pltpu.make_async_remote_copy(
        src_ref=src,
        dst_ref=dst,
        send_sem=send_sem,
        recv_sem=recv_sem,
        device_id=where,
        device_id_type=pl.DeviceIdType.MESH,
    ).start()


def wait_for(ref, sem):
    pltpu.make_async_copy(ref, ref, sem).wait()


def selection(quarter, y, core, fl_ref, pt_ref, ow_ref, s_mat):
    ii = lax.broadcasted_iota(jnp.int32, (TILE, TILE), 0)
    jj = lax.broadcasted_iota(jnp.int32, (TILE, TILE), 1)

    def row(values):
        return jnp.broadcast_to(values.astype(F32), (TILE, TILE))

    own = row(ow_ref[...])
    own_c = own.T
    rank = jnp.sum(jnp.where((own_c == own) & (jj < ii), 1.0, 0.0), axis=1, keepdims=True)
    owner_y = (y + core + 2 * ((jj % 32) // NZ)) % NY
    holder = ((owner_y * NZ + jj % NZ) * 2 + jj // 64).astype(F32)
    order = ((jj // 32) % 2).astype(F32)
    chosen = jnp.where((own_c == holder) & (rank == order), 1.0, 0.0)
    a = jnp.sum(chosen * (row(pt_ref[0:1, :]).T + 1.0), axis=0, keepdims=True) - 1.0
    t = jnp.sum(chosen * (row(pt_ref[1:2, :]).T + 1.0), axis=0, keepdims=True) - 1.0
    tiles = ii.astype(F32)
    flags_a, flags_t = [], []
    for w in range(2):
        fc = row(fl_ref[w : w + 1, :]).T
        flags_a.append(jnp.sum(jnp.where(tiles == a, fc, 0.0), axis=0, keepdims=True))
        flags_t.append(jnp.sum(jnp.where(tiles == t, fc, 0.0), axis=0, keepdims=True))
    together = flags_a[0] * flags_t[0] + flags_a[1] * flags_t[1]
    share = jnp.where(together > 1.5, 0.5, 1.0)
    first = (quarter * TQ).astype(F32)
    a_here = a - first
    t_here = t - first
    low, mid = ii < 32, ii < 96
    part = jnp.where(low, ii // 8, jnp.where(mid, (ii - 32) // 16, (ii - 96) // 8))
    tile = jnp.where(low, ii % 8, jnp.where(mid, 8 + ii % 16, 24 + ii % 8)).astype(F32)
    edge_part = jnp.where(low, ii // 8, jnp.where(ii < 64, (ii - 32) // 8, -1))
    edge_tile = jnp.where(low, ii % 8 - 8, 32 + ii % 8).astype(F32)
    for p in range(4):
        w = p // 2
        left = pl.ds(p * TILE, TILE)
        right = pl.ds((4 + p) * TILE, TILE)
        here = part == p
        s_mat[0:TILE, left] = jnp.where(
            here & (tile == a_here), flags_a[w] * share, 0.0
        ).astype(BF)
        s_mat[0:TILE, right] = jnp.where(here & (tile == t_here), flags_t[w], 0.0).astype(BF)
        s_mat[TILE : 2 * TILE, left] = jnp.zeros((TILE, TILE), BF)
        s_mat[TILE : 2 * TILE, right] = jnp.where(
            (edge_part == p) & (edge_tile == t_here), flags_t[w], 0.0
        ).astype(BF)


def kernel(
    x_hbm, fl_hbm, pt_hbm, ow_hbm, w_hbm, out_ref,
    x_v, fl_v, pt_v, ow_v, w_v, a_f, b_f, b_k, x_in, m, r, hs, h, s_mat, acc, y_f, y_h, q_h, ps, pr,
    in_sems, w_sem, pre_send, pre_recv, send1, recv1, sib_send, sib_recv, edge_send, edge_recv,
    send2, recv2, post_send, post_recv,
):
    band = lax.axis_index("band")
    quarter = lax.axis_index("chan")
    chip, core = band // 2, band % 2
    y, z = chip // NZ, chip % NZ
    other = chip * 2 + 1 - core
    up, down = quarter + 1, quarter - 1
    has_up, has_down = quarter < QUARTERS - 1, quarter > 0

    barrier = pltpu.get_barrier_semaphore()

    def greet(to_band, to_chan):
        pl.semaphore_signal(
            barrier, inc=1, device_id=(to_band, to_chan), device_id_type=pl.DeviceIdType.MESH
        )

    def row_of(who, j):
        return (y + who + 2 * j) % NY

    def step(i):
        return jnp.where(i % 2 == 1, NZ // 2 - (i + 1) // 2, NZ // 2 + i // 2)

    @pl.loop(0, NZ)
    def _(i):
        for j in range(2):
            g = row_of(core, j) * NZ + (z + step(i)) % NZ

            @pl.when(g != chip)
            def _():
                greet(g * 2 + core, quarter)

    loads = [
        pltpu.make_async_copy(x_hbm, x_v, in_sems.at[0]),
        pltpu.make_async_copy(fl_hbm, fl_v, in_sems.at[1]),
        pltpu.make_async_copy(pt_hbm, pt_v, in_sems.at[2]),
        pltpu.make_async_copy(ow_hbm, ow_v, in_sems.at[3]),
    ]
    for load in loads:
        load.start()
    load_w = pltpu.make_async_copy(w_hbm, w_v, w_sem)
    load_w.start()

    greet(other, quarter)
    for there, beside in ((has_up, up), (has_down, down)):

        @pl.when(there)
        def _():
            greet(band, beside)
            greet(other, beside)

    for load in loads:
        load.wait()

    for tile in range(TQ):
        lanes = pl.ds(tile * TILE, TILE)
        for w in range(2):
            re = x_v[2 * w, :, lanes].astype(F32)
            im = x_v[2 * w + 1, :, lanes].astype(F32)
            energy = jnp.sum(re * re + im * im, axis=0, keepdims=True)
            scale = lax.rsqrt(energy * (1.0 / BINS) + FLOOR)
            a_f[pl.ds(8 * place(tile, 2 * w), 8), :] = re * scale
            a_f[pl.ds(8 * place(tile, 2 * w + 1), 8), :] = im * scale
    for i in range(BINS):
        b_f[pl.ds(i, TILE, stride=BINS), :] = a_f[pl.ds(i, TILE, stride=BINS), :].T
    def round_batch(b):
        rows = b_f[...].reshape(CHIPS, 2, BINS, TILE)[:, b]
        b_k[b] = rows.reshape(NY, 8, 16, TILE).astype(BF)

    round_batch(0)
    pl.semaphore_wait(
        barrier, 32 + core + 2 * has_up.astype(jnp.int32) + 2 * has_down.astype(jnp.int32)
    )

    for b in range(2):
        if b == 1:
            round_batch(1)
        for j in range(2):
            send(
                b_k.at[b, row_of(1 - core, j)], x_in.at[b, j], pre_send, pre_recv.at[b],
                (other, quarter),
            )

    def merge(b):
        wait_for(x_in.at[b], pre_recv.at[b])
        for j in range(2):
            rows = b_f[pl.ds(row_of(core, j) * 256, 256), :]
            own = rows.reshape(NZ, 2, BINS, TILE)[:, b]
            theirs = x_in[b, j].astype(F32).reshape(NZ, BINS, TILE)
            low = jnp.where(core == 0, own, theirs)
            high = jnp.where(core == 0, theirs, own)
            both = jnp.stack([low, high], axis=1)
            m[b, j] = both.reshape(NZ, 16, TILE).astype(BF)

    def dispatch(src, dst, b, j, send_sem, recv_sem):
        to_y = row_of(core, j)
        there = (j + core) % 2

        @pl.loop(0, NZ)
        def _(i):
            to_z = (z + step(i)) % NZ
            g = to_y * NZ + to_z

            @pl.when(g != chip)
            def _():
                send(
                    src.at[b, j, to_z], dst.at[2 * b + there, z], send_sem, recv_sem(there),
                    (g * 2 + core, quarter),
                )

        if j == 0:

            @pl.when(core == 0)
            def _():
                pltpu.make_async_copy(src.at[b, 0, z], dst.at[2 * b, z], recv_sem(0)).start()

    def left(src, b, j, send_sem):
        wait_for(src.at[b, j, pl.ds(0, NZ - 1)], send_sem)
        if j == 0:

            @pl.when(core == 1)
            def _():
                wait_for(src.at[b, j, 0], send_sem)

        else:
            wait_for(src.at[b, j, 0], send_sem)

    merge(0)
    for j in range(2):
        dispatch(m, r.at[0], 0, j, send1.at[j], lambda there: recv1.at[there])
    merge(1)
    selection(quarter, y, core, fl_v, pt_v, ow_v, s_mat)
    acc[...] = jnp.zeros_like(acc)
    for d, there in ((0, has_down), (1, has_up)):

        @pl.when(jnp.logical_not(there))
        def _():
            h[:, d] = jnp.zeros((4, 2, 64, TILE), BF)

    left(m, 0, 0, send1.at[0])
    dispatch(m, r.at[0], 1, 0, send1.at[2], lambda there: recv1.at[2 + there])
    load_w.wait()

    block = lax.broadcasted_iota(jnp.int32, (64, TILE), 1) // 32

    def arrive(t):
        wait_for(r.at[0, t], recv1.at[t])
        send(r.at[0, t], r.at[1, t], sib_send, sib_recv.at[t], (other, quarter))
        rows = r[0, t].reshape(4, 64, TILE).astype(F32)
        high = rows[3]
        low = rows[0]
        for q in range(3):
            high = jnp.where(block == q, pltpu.roll(rows[q], (32 * q + 32) % TILE, 1), high)
        for q in range(1, 4):
            low = jnp.where(block == q, pltpu.roll(rows[q], 32 * q, 1), low)
        hs[t, 0] = high.astype(BF)
        hs[t, 1] = low.astype(BF)
        for d, there, beside in ((0, has_up, up), (1, has_down, down)):

            @pl.when(there)
            def _():
                send(hs.at[t, d], h.at[t, d, 0], edge_send.at[d], edge_recv.at[t, d], (band, beside))
                send(hs.at[t, d], h.at[t, d, 1], edge_send.at[d], edge_recv.at[t, d], (other, beside))

    def compute(t):
        for d, there in ((0, has_down), (1, has_up)):

            @pl.when(there)
            def _():
                wait_for(h.at[t, d], edge_recv.at[t, d])

        wait_for(r.at[1, t], sib_recv.at[t])
        total = None
        for o in range(2):
            from_low = h[t, 0, o].astype(F32)
            from_high = h[t, 1, o].astype(F32)
            edge = jnp.concatenate(
                [
                    jnp.where(
                        block == 0,
                        pltpu.roll(from_low, (TILE - 32 * q) % TILE, 1) if q else from_low,
                        pltpu.roll(from_high, (TILE + 32 - 32 * q) % TILE, 1)
                        if q != 1
                        else from_high,
                    )
                    for q in range(4)
                ],
                axis=0,
            ).astype(BF)
            rows = jnp.concatenate([r[o, t].reshape(2 * TILE, TILE), edge], axis=1)
            g = jnp.dot(rows, s_mat[...], preferred_element_type=F32)
            left = [g[:, p * TILE : (p + 1) * TILE] for p in range(4)]
            right = [g[:, (4 + p) * TILE : (5 + p) * TILE] for p in range(4)]
            re = (left[0] * right[0] + left[1] * right[1]) + (
                left[2] * right[2] + left[3] * right[3]
            )
            im = (left[0] * right[1] - left[1] * right[0]) + (
                left[2] * right[3] - left[3] * right[2]
            )
            cross = jnp.concatenate([re, im], axis=0).astype(BF)
            index = row_of(core if o == 0 else 1 - core, t % 2)
            part = jnp.dot(w_v[index], cross, preferred_element_type=F32)
            total = part if total is None else total + part
        acc[t // 2] += total

    def finish(b):
        for c in range(4):
            turned = acc[b, c * TILE : (c + 1) * TILE, :].T
            for s in range(4):
                y_f[pl.ds(s * 4 + c, 32, stride=16), :] = turned[s * 32 : (s + 1) * 32]
        y_h[b] = y_f[...].astype(BF).reshape(2, NZ, 16, TILE)
        for j in range(2):
            dispatch(y_h, q_h, b, j, send2.at[b, j], lambda there: recv2.at[2 * b + there])

    def put(values, t, who):
        first = row_of(who, t % 2) * 256 + t // 2 * 8
        for i in range(NZ):
            a_f[pl.ds(pl.multiple_of(first + i * 16, 8), 8), :] = values[i]

    def collect(t):
        wait_for(q_h.at[t], recv2.at[t])
        got = q_h[t].astype(F32).reshape(NZ, 2, 8, TILE)
        theirs = jnp.where(core == 0, got[:, 1], got[:, 0])
        ps[t] = theirs.reshape(8, 16, TILE).astype(BF)
        send(ps.at[t], pr.at[t], post_send, post_recv.at[t], (other, quarter))
        put(jnp.where(core == 0, got[:, 0], got[:, 1]), t, core)

    def join(t):
        wait_for(pr.at[t], post_recv.at[t])
        put(pr[t].astype(F32).reshape(NZ, 8, TILE), t, 1 - core)

    arrive(0)
    left(m, 0, 1, send1.at[1])
    dispatch(m, r.at[0], 1, 1, send1.at[3], lambda there: recv1.at[2 + there])
    arrive(1)
    compute(0)
    compute(1)
    finish(0)
    arrive(2)
    arrive(3)
    compute(2)
    compute(3)
    finish(1)
    for t in range(4):
        collect(t)
        if t >= 1:
            join(t - 1)
    join(3)
    for s in range(2):
        for c in range(4):
            out_ref[s, c * TILE : (c + 1) * TILE, :] = a_f[
                pl.ds(s * 4 + c, TILE, stride=BINS), :
            ].T

    for j in range(2):
        left(m, 1, j, send1.at[2 + j])
        for b in range(2):
            left(y_h, b, j, send2.at[b, j])
    wait_for(x_in, pre_send)
    wait_for(r.at[0], sib_send)
    wait_for(ps, post_send)
    for d, there in ((0, has_up), (1, has_down)):

        @pl.when(there)
        def _():
            wait_for(h.at[:, d], edge_send.at[d])


def body(spectra, window_flags, pair_tiles, owners, stacks):
    x = jnp.transpose(spectra, (0, 1, 3, 2)).reshape(4, BINS, TQ * TILE)
    pairs = pair_tiles[0].T
    held = owners[0].T
    table = jnp.asarray(lag_table())
    dma = pltpu.SemaphoreType.DMA
    added = pl.pallas_call(
        kernel,
        out_shape=jax.ShapeDtypeStruct((2, LAGS, TILE), F32),
        in_specs=[pl.BlockSpec(memory_space=pltpu.HBM)] * 5,
        out_specs=pl.BlockSpec(memory_space=pltpu.VMEM),
        scratch_shapes=[
            pltpu.VMEM((4, BINS, TQ * TILE), BF),
            pltpu.VMEM((2, TILE), jnp.int32),
            pltpu.VMEM((2, TILE), jnp.int32),
            pltpu.VMEM((1, TILE), jnp.int32),
            pltpu.VMEM((NY, LAGS, 512), BF),
            pltpu.VMEM((1024, TILE), F32),
            pltpu.VMEM((1024, TILE), F32),
            pltpu.VMEM((2, NY, 8, 16, TILE), BF),
            pltpu.VMEM((2, 2, 8, 16, TILE), BF),
            pltpu.VMEM((2, 2, NZ, 16, TILE), BF),
            pltpu.VMEM((2, 4, NZ, 16, TILE), BF),
            pltpu.VMEM((4, 2, 64, TILE), BF),
            pltpu.VMEM((4, 2, 2, 64, TILE), BF),
            pltpu.VMEM((256, 1024), BF),
            pltpu.VMEM((2, LAGS, TILE), F32),
            pltpu.VMEM((512, TILE), F32),
            pltpu.VMEM((2, 2, NZ, 16, TILE), BF),
            pltpu.VMEM((4, NZ, 16, TILE), BF),
            pltpu.VMEM((4, 8, 16, TILE), BF),
            pltpu.VMEM((4, 8, 16, TILE), BF),
            dma((4,)),
            dma(()),
            dma(()),
            dma((2,)),
            dma((4,)),
            dma((4,)),
            dma(()),
            dma((4,)),
            dma((2,)),
            dma((4, 2)),
            dma((2, 2)),
            dma((4,)),
            dma(()),
            dma((4,)),
        ],
        compiler_params=pltpu.CompilerParams(
            collective_id=0, has_side_effects=True, vmem_limit_bytes=32 << 20
        ),
    )(
        *(
            pltpu.with_memory_space_constraint(v, pltpu.HBM)
            for v in (x, window_flags, pairs, held, table)
        )
    )
    return stacks + added[None]


def solution(mesh):
    in_specs = (
        P(None, None, "chan", "band"),
        P(),
        P("chan", None, None),
        P("chan", None, None),
        P("chan", "band", None, None),
    )
    out_specs = P("chan", "band", None, None)
    return jax.shard_map(body, mesh=mesh, in_specs=in_specs, out_specs=out_specs, check_vma=False)
```

```python
import math

import jax
import jax.numpy as jnp
import numpy as np
from jax import lax
from jax.experimental import pallas as pl
from jax.experimental.pallas import tpu as pltpu
from jax.sharding import PartitionSpec as P

TILE = 128
LAGS = 512
NF = 1024
NY, NZ = 4, 16
CHIPS = NY * NZ
QUARTERS = 4
TQ = 32
BINS = 8
FLOOR = 1e-05
BF = jnp.bfloat16
F32 = jnp.float32


def lag_table():
    tau = np.arange(LAGS) - LAGS // 2
    phase = np.mod(tau[:, None] * np.arange(NF)[None, :], NF)
    angles = phase.astype(np.float32) * np.float32(2.0 * math.pi / NF)
    amplitude = np.float32(1.0 / math.sqrt(NF))
    both = np.stack([np.cos(angles) * amplitude, -np.sin(angles) * amplitude])
    both = both.astype(np.float32).astype(jnp.bfloat16)
    both = both.reshape(2, LAGS, NY, NZ * 2 * BINS)
    return both.transpose(2, 1, 0, 3).reshape(NY, LAGS, 4 * NZ * BINS)


def place(tile, part):
    if tile < 8:
        return part * 8 + tile
    if tile < 24:
        return 32 + part * 16 + tile - 8
    return 96 + part * 8 + tile - 24


def send(src, dst, send_sem, recv_sem, where):
    pltpu.make_async_remote_copy(
        src_ref=src,
        dst_ref=dst,
        send_sem=send_sem,
        recv_sem=recv_sem,
        device_id=where,
        device_id_type=pl.DeviceIdType.MESH,
    ).start()


def wait_for(ref, sem):
    pltpu.make_async_copy(ref, ref, sem).wait()


def selection(quarter, y, core, fl_ref, pt_ref, ow_ref, s_mat):
    ii = lax.broadcasted_iota(jnp.int32, (TILE, TILE), 0)
    jj = lax.broadcasted_iota(jnp.int32, (TILE, TILE), 1)

    def row(values):
        return jnp.broadcast_to(values.astype(F32), (TILE, TILE))

    own = row(ow_ref[...])
    own_c = own.T
    rank = jnp.sum(jnp.where((own_c == own) & (jj < ii), 1.0, 0.0), axis=1, keepdims=True)
    owner_y = (y + core + 2 * ((jj % 32) // NZ)) % NY
    holder = ((owner_y * NZ + jj % NZ) * 2 + jj // 64).astype(F32)
    order = ((jj // 32) % 2).astype(F32)
    chosen = jnp.where((own_c == holder) & (rank == order), 1.0, 0.0)
    a = jnp.sum(chosen * (row(pt_ref[0:1, :]).T + 1.0), axis=0, keepdims=True) - 1.0
    t = jnp.sum(chosen * (row(pt_ref[1:2, :]).T + 1.0), axis=0, keepdims=True) - 1.0
    tiles = ii.astype(F32)
    flags_a, flags_t = [], []
    for w in range(2):
        fc = row(fl_ref[w : w + 1, :]).T
        flags_a.append(jnp.sum(jnp.where(tiles == a, fc, 0.0), axis=0, keepdims=True))
        flags_t.append(jnp.sum(jnp.where(tiles == t, fc, 0.0), axis=0, keepdims=True))
    together = flags_a[0] * flags_t[0] + flags_a[1] * flags_t[1]
    share = jnp.where(together > 1.5, 0.5, 1.0)
    first = (quarter * TQ).astype(F32)
    a_here = a - first
    t_here = t - first
    low, mid = ii < 32, ii < 96
    part = jnp.where(low, ii // 8, jnp.where(mid, (ii - 32) // 16, (ii - 96) // 8))
    tile = jnp.where(low, ii % 8, jnp.where(mid, 8 + ii % 16, 24 + ii % 8)).astype(F32)
    edge_part = jnp.where(low, ii // 8, jnp.where(ii < 64, (ii - 32) // 8, -1))
    edge_tile = jnp.where(low, ii % 8 - 8, 32 + ii % 8).astype(F32)
    for p in range(4):
        w = p // 2
        left = pl.ds(p * TILE, TILE)
        right = pl.ds((4 + p) * TILE, TILE)
        here = part == p
        s_mat[0:TILE, left] = jnp.where(
            here & (tile == a_here), flags_a[w] * share, 0.0
        ).astype(BF)
        s_mat[0:TILE, right] = jnp.where(here & (tile == t_here), flags_t[w], 0.0).astype(BF)
        s_mat[TILE : 2 * TILE, left] = jnp.zeros((TILE, TILE), BF)
        s_mat[TILE : 2 * TILE, right] = jnp.where(
            (edge_part == p) & (edge_tile == t_here), flags_t[w], 0.0
        ).astype(BF)


def kernel(
    x_hbm, fl_hbm, pt_hbm, ow_hbm, w_hbm, out_ref,
    x_v, fl_v, pt_v, ow_v, w_v, a_f, b_f, b_k, x_in, m, r, hs, h, s_mat, acc, y_f, y_h, q_h, ps, pr,
    in_sems, w_sem, pre_send, pre_recv, send1, recv1, sib_send, sib_recv, edge_send, edge_recv,
    send2, recv2, post_send, post_recv,
):
    band = lax.axis_index("band")
    quarter = lax.axis_index("chan")
    chip, core = band // 2, band % 2
    y, z = chip // NZ, chip % NZ
    other = chip * 2 + 1 - core
    up, down = quarter + 1, quarter - 1
    has_up, has_down = quarter < QUARTERS - 1, quarter > 0

    barrier = pltpu.get_barrier_semaphore()

    def greet(to_band, to_chan):
        pl.semaphore_signal(
            barrier, inc=1, device_id=(to_band, to_chan), device_id_type=pl.DeviceIdType.MESH
        )

    def row_of(who, j):
        return (y + who + 2 * j) % NY

    def step(i):
        return jnp.where(i % 2 == 1, NZ // 2 - (i + 1) // 2, NZ // 2 + i // 2)

    @pl.loop(0, NZ)
    def _(i):
        for j in range(2):
            g = row_of(core, j) * NZ + (z + step(i)) % NZ

            @pl.when(g != chip)
            def _():
                greet(g * 2 + core, quarter)

    loads = [
        pltpu.make_async_copy(x_hbm, x_v, in_sems.at[0]),
        pltpu.make_async_copy(fl_hbm, fl_v, in_sems.at[1]),
        pltpu.make_async_copy(pt_hbm, pt_v, in_sems.at[2]),
        pltpu.make_async_copy(ow_hbm, ow_v, in_sems.at[3]),
    ]
    for load in loads:
        load.start()
    load_w = pltpu.make_async_copy(w_hbm, w_v, w_sem)
    load_w.start()

    greet(other, quarter)
    for there, beside in ((has_up, up), (has_down, down)):

        @pl.when(there)
        def _():
            greet(band, beside)
            greet(other, beside)

    for load in loads:
        load.wait()

    for tile in range(TQ):
        lanes = pl.ds(tile * TILE, TILE)
        for w in range(2):
            re = x_v[2 * w, :, lanes].astype(F32)
            im = x_v[2 * w + 1, :, lanes].astype(F32)
            energy = jnp.sum(re * re + im * im, axis=0, keepdims=True)
            scale = lax.rsqrt(energy * (1.0 / BINS) + FLOOR)
            a_f[pl.ds(8 * place(tile, 2 * w), 8), :] = re * scale
            a_f[pl.ds(8 * place(tile, 2 * w + 1), 8), :] = im * scale
    for i in range(BINS):
        b_f[pl.ds(i, TILE, stride=BINS), :] = a_f[pl.ds(i, TILE, stride=BINS), :].T
    def round_batch(b):
        rows = b_f[...].reshape(CHIPS, 2, BINS, TILE)[:, b]
        b_k[b] = rows.reshape(NY, 8, 16, TILE).astype(BF)

    round_batch(0)
    pl.semaphore_wait(
        barrier, 32 + core + 2 * has_up.astype(jnp.int32) + 2 * has_down.astype(jnp.int32)
    )

    for b in range(2):
        if b == 1:
            round_batch(1)
        for j in range(2):
            send(
                b_k.at[b, row_of(1 - core, j)], x_in.at[b, j], pre_send, pre_recv.at[b],
                (other, quarter),
            )

    def merge(b):
        wait_for(x_in.at[b], pre_recv.at[b])
        for j in range(2):
            rows = b_f[pl.ds(row_of(core, j) * 256, 256), :]
            own = rows.reshape(NZ, 2, BINS, TILE)[:, b]
            theirs = x_in[b, j].astype(F32).reshape(NZ, BINS, TILE)
            low = jnp.where(core == 0, own, theirs)
            high = jnp.where(core == 0, theirs, own)
            both = jnp.stack([low, high], axis=1)
            m[b, j] = both.reshape(NZ, 16, TILE).astype(BF)

    def dispatch(src, dst, b, j, send_sem, recv_sem):
        to_y = row_of(core, j)
        there = (j + core) % 2

        @pl.loop(0, NZ)
        def _(i):
            to_z = (z + step(i)) % NZ
            g = to_y * NZ + to_z

            @pl.when(g != chip)
            def _():
                send(
                    src.at[b, j, to_z], dst.at[2 * b + there, z], send_sem, recv_sem(there),
                    (g * 2 + core, quarter),
                )

        if j == 0:

            @pl.when(core == 0)
            def _():
                pltpu.make_async_copy(src.at[b, 0, z], dst.at[2 * b, z], recv_sem(0)).start()

    def left(src, b, j, send_sem):
        wait_for(src.at[b, j, pl.ds(0, NZ - 1)], send_sem)
        if j == 0:

            @pl.when(core == 1)
            def _():
                wait_for(src.at[b, j, 0], send_sem)

        else:
            wait_for(src.at[b, j, 0], send_sem)

    merge(0)
    for j in range(2):
        dispatch(m, r.at[0], 0, j, send1.at[j], lambda there: recv1.at[there])
    merge(1)
    selection(quarter, y, core, fl_v, pt_v, ow_v, s_mat)
    acc[...] = jnp.zeros_like(acc)
    for d, there in ((0, has_down), (1, has_up)):

        @pl.when(jnp.logical_not(there))
        def _():
            h[:, d] = jnp.zeros((4, 2, 64, TILE), BF)

    left(m, 0, 0, send1.at[0])
    dispatch(m, r.at[0], 1, 0, send1.at[2], lambda there: recv1.at[2 + there])
    load_w.wait()

    block = lax.broadcasted_iota(jnp.int32, (64, TILE), 1) // 32

    def arrive(t):
        wait_for(r.at[0, t], recv1.at[t])
        send(r.at[0, t], r.at[1, t], sib_send, sib_recv.at[t], (other, quarter))
        rows = r[0, t].reshape(4, 64, TILE).astype(F32)
        high = rows[3]
        low = rows[0]
        for q in range(3):
            high = jnp.where(block == q, pltpu.roll(rows[q], (32 * q + 32) % TILE, 1), high)
        for q in range(1, 4):
            low = jnp.where(block == q, pltpu.roll(rows[q], 32 * q, 1), low)
        hs[t, 0] = high.astype(BF)
        hs[t, 1] = low.astype(BF)
        for o, core_to in ((0, band), (1, other)):
            for d, there, beside in ((0, has_up, up), (1, has_down, down)):

                @pl.when(there)
                def _():
                    send(
                        hs.at[t, d], h.at[t, d, o], edge_send.at[d], edge_recv.at[t, d, o],
                        (core_to, beside),
                    )

    def compute(t, halves=(0, 1)):
        total = None
        for o in halves:
            if o == 1:
                wait_for(r.at[1, t], sib_recv.at[t])
            for d, there in ((0, has_down), (1, has_up)):

                @pl.when(there)
                def _():
                    wait_for(h.at[t, d, o], edge_recv.at[t, d, o])

            from_low = h[t, 0, o].astype(F32)
            from_high = h[t, 1, o].astype(F32)
            edge = jnp.concatenate(
                [
                    jnp.where(
                        block == 0,
                        pltpu.roll(from_low, (TILE - 32 * q) % TILE, 1) if q else from_low,
                        pltpu.roll(from_high, (TILE + 32 - 32 * q) % TILE, 1)
                        if q != 1
                        else from_high,
                    )
                    for q in range(4)
                ],
                axis=0,
            ).astype(BF)
            rows = jnp.concatenate([r[o, t].reshape(2 * TILE, TILE), edge], axis=1)
            g = jnp.dot(rows, s_mat[...], preferred_element_type=F32)
            left = [g[:, p * TILE : (p + 1) * TILE] for p in range(4)]
            right = [g[:, (4 + p) * TILE : (5 + p) * TILE] for p in range(4)]
            re = (left[0] * right[0] + left[1] * right[1]) + (
                left[2] * right[2] + left[3] * right[3]
            )
            im = (left[0] * right[1] - left[1] * right[0]) + (
                left[2] * right[3] - left[3] * right[2]
            )
            cross = jnp.concatenate([re, im], axis=0).astype(BF)
            index = row_of(core if o == 0 else 1 - core, t % 2)
            part = jnp.dot(w_v[index], cross, preferred_element_type=F32)
            total = part if total is None else total + part
        acc[t // 2] += total

    def finish(b):
        for c in range(4):
            turned = acc[b, c * TILE : (c + 1) * TILE, :].T
            for s in range(4):
                y_f[pl.ds(s * 4 + c, 32, stride=16), :] = turned[s * 32 : (s + 1) * 32]
        y_h[b] = y_f[...].astype(BF).reshape(2, NZ, 16, TILE)
        for j in range(2):
            dispatch(y_h, q_h, b, j, send2.at[b, j], lambda there: recv2.at[2 * b + there])

    def put(values, t, who):
        first = row_of(who, t % 2) * 256 + t // 2 * 8
        for i in range(NZ):
            a_f[pl.ds(pl.multiple_of(first + i * 16, 8), 8), :] = values[i]

    def collect(t):
        wait_for(q_h.at[t], recv2.at[t])
        got = q_h[t].astype(F32).reshape(NZ, 2, 8, TILE)
        theirs = jnp.where(core == 0, got[:, 1], got[:, 0])
        ps[t] = theirs.reshape(8, 16, TILE).astype(BF)
        send(ps.at[t], pr.at[t], post_send, post_recv.at[t], (other, quarter))
        put(jnp.where(core == 0, got[:, 0], got[:, 1]), t, core)

    def join(t):
        wait_for(pr.at[t], post_recv.at[t])
        put(pr[t].astype(F32).reshape(NZ, 8, TILE), t, 1 - core)

    arrive(0)
    left(m, 0, 1, send1.at[1])
    dispatch(m, r.at[0], 1, 1, send1.at[3], lambda there: recv1.at[2 + there])
    arrive(1)
    for o in range(2):
        compute(0, (o,))
        compute(1, (o,))
    finish(0)
    arrive(2)
    arrive(3)
    for o in range(2):
        compute(2, (o,))
        compute(3, (o,))
    finish(1)
    for t in range(4):
        collect(t)
        if t >= 1:
            join(t - 1)
    join(3)
    for s in range(2):
        for c in range(4):
            out_ref[s, c * TILE : (c + 1) * TILE, :] = a_f[
                pl.ds(s * 4 + c, TILE, stride=BINS), :
            ].T

    for j in range(2):
        left(m, 1, j, send1.at[2 + j])
        for b in range(2):
            left(y_h, b, j, send2.at[b, j])
    wait_for(x_in, pre_send)
    wait_for(r.at[0], sib_send)
    wait_for(ps, post_send)
    for d, there in ((0, has_up), (1, has_down)):

        @pl.when(there)
        def _():
            wait_for(h.at[:, d], edge_send.at[d])


def body(spectra, window_flags, pair_tiles, owners, stacks):
    x = jnp.transpose(spectra, (0, 1, 3, 2)).reshape(4, BINS, TQ * TILE)
    pairs = pair_tiles[0].T
    held = owners[0].T
    table = jnp.asarray(lag_table())
    dma = pltpu.SemaphoreType.DMA
    added = pl.pallas_call(
        kernel,
        out_shape=jax.ShapeDtypeStruct((2, LAGS, TILE), F32),
        in_specs=[pl.BlockSpec(memory_space=pltpu.HBM)] * 5,
        out_specs=pl.BlockSpec(memory_space=pltpu.VMEM),
        scratch_shapes=[
            pltpu.VMEM((4, BINS, TQ * TILE), BF),
            pltpu.VMEM((2, TILE), jnp.int32),
            pltpu.VMEM((2, TILE), jnp.int32),
            pltpu.VMEM((1, TILE), jnp.int32),
            pltpu.VMEM((NY, LAGS, 512), BF),
            pltpu.VMEM((1024, TILE), F32),
            pltpu.VMEM((1024, TILE), F32),
            pltpu.VMEM((2, NY, 8, 16, TILE), BF),
            pltpu.VMEM((2, 2, 8, 16, TILE), BF),
            pltpu.VMEM((2, 2, NZ, 16, TILE), BF),
            pltpu.VMEM((2, 4, NZ, 16, TILE), BF),
            pltpu.VMEM((4, 2, 64, TILE), BF),
            pltpu.VMEM((4, 2, 2, 64, TILE), BF),
            pltpu.VMEM((256, 1024), BF),
            pltpu.VMEM((2, LAGS, TILE), F32),
            pltpu.VMEM((512, TILE), F32),
            pltpu.VMEM((2, 2, NZ, 16, TILE), BF),
            pltpu.VMEM((4, NZ, 16, TILE), BF),
            pltpu.VMEM((4, 8, 16, TILE), BF),
            pltpu.VMEM((4, 8, 16, TILE), BF),
            dma((4,)),
            dma(()),
            dma(()),
            dma((2,)),
            dma((4,)),
            dma((4,)),
            dma(()),
            dma((4,)),
            dma((2,)),
            dma((4, 2, 2)),
            dma((2, 2)),
            dma((4,)),
            dma(()),
            dma((4,)),
        ],
        compiler_params=pltpu.CompilerParams(
            collective_id=0, has_side_effects=True, vmem_limit_bytes=32 << 20
        ),
    )(
        *(
            pltpu.with_memory_space_constraint(v, pltpu.HBM)
            for v in (x, window_flags, pairs, held, table)
        )
    )
    return stacks + added[None]


def solution(mesh):
    in_specs = (
        P(None, None, "chan", "band"),
        P(),
        P("chan", None, None),
        P("chan", None, None),
        P("chan", "band", None, None),
    )
    out_specs = P("chan", "band", None, None)
    return jax.shard_map(body, mesh=mesh, in_specs=in_specs, out_specs=out_specs, check_vma=False)
```
